128 devices in a mesh: lon: 16 (over y_hi, x, core), lat: 8 (over z, y_lo).
Axes of the slice: x: 4, y: 4 (y_hi: 2, y_lo: 2; y = y_hi * 2 + y_lo), z: 4, core: 2. Of those that a mesh axis runs over, the one named last changes fastest.
Arguments:
- fields: bfloat16 [4, 48, 384, 192], P(None, 'lat', 'lon'), may hold values from -6 to 6
- cotangent: bfloat16 [4, 48, 384, 192], P(None, 'lat', 'lon'), may hold values from -6 to 6
- window_kinds: int32 [2, 8], P(None, 'lat'), may hold values from 0 to 15
- first_gain: float32 [192], replicated, may hold values from 0.1 to 1.9
- attend_weight: bfloat16 [192, 576], replicated, may hold values from -0.4375 to 0.4375
- output_weight: bfloat16 [192, 192], replicated, may hold values from -0.4375 to 0.4375
- second_gain: float32 [192], replicated, may hold values from 0.1 to 1.9
- expand_weight: bfloat16 [192, 768], replicated, may hold values from -0.4375 to 0.4375
- shrink_weight: bfloat16 [768, 192], replicated, may hold values from -0.21875 to 0.21875
- bias_table: float32 [16, 6, 3312], replicated, may hold values from -3 to 360
Outputs:
- grad_fields: bfloat16 [4, 48, 384, 192], P(None, 'lat', 'lon')
- grad_first_gain: float32 [192], replicated
- grad_attend_weight: float32 [192, 576], replicated
- grad_output_weight: float32 [192, 192], replicated
- grad_second_gain: float32 [192], replicated
- grad_expand_weight: float32 [192, 768], replicated
- grad_shrink_weight: float32 [768, 192], replicated
- grad_bias_table: float32 [16, 6, 3312], replicated
The draws below stay inside these ranges and needn't reach their ends.
All inputs are finite; a program needn't handle non-finite values.
Results may differ from the reference program's by a relative error of at most 0.02.
Values may be sent and summed in bfloat16 or wider, within the bound.
A program may use at most 256 MiB of HBM per device.

```python
import math
import jax
import jax.numpy as jnp
import numpy as np
from jax import lax

C = 192
HEADS = 6
HID = 768
WZ = 2
WLAT = 6
WLON = 12
LEV = 4
POS = 3312
NLAT = 48
NLON = 384
TYPES = 16


def draw_fields(key, part):
    key = jax.random.fold_in(key, 11)
    grid_shape = (LEV, NLAT, NLON, C)
    sampled = jnp.clip(jax.random.normal(key, grid_shape, jnp.float32), -6.0, 6.0)
    return sampled.astype(jnp.bfloat16)


def draw_bias_table(key, part):
    key = jax.random.fold_in(key, 23)
    table_shape = (TYPES, HEADS, POS)
    sampled = jnp.clip(jax.random.normal(key, table_shape, jnp.float32), -3.0, 3.0)
    return sampled


def touch_ends(result, key, least, high):
    dims = result.shape
    spot = [jax.random.randint(jax.random.fold_in(key, axis), (), 0, dims[axis]) for axis in range(len(dims))]
    result = result.at[tuple(spot)].set(least)
    longest = dims.index(max(dims))
    spot[longest] = (spot[longest] + 1) % dims[longest]
    return result.at[tuple(spot)].set(high)


def block_levels(own_key, extent, cuts, low, high):
    factor_of, own = 1.0, jax.random.fold_in(own_key, 6)
    for axis_at, shards_of in cuts:
        heights = jnp.exp(jax.random.uniform(jax.random.fold_in(own, axis_at), (shards_of,), jnp.float32, low / len(cuts), high / len(cuts)))
        factor_of = factor_of * jnp.repeat(heights, extent[axis_at] // shards_of).reshape([-1 if axis == axis_at else 1 for axis in range(len(extent))])
    return factor_of


def bell_draw(own_key, extent, width, limit, cuts=(), kind=jnp.bfloat16):
    entries = width * jax.random.normal(own_key, extent, jnp.float32)
    if cuts:
        entries = entries * block_levels(own_key, extent, cuts, -0.22, 0.18)
    return jnp.clip(entries, -limit, limit).astype(kind)


def setup_inputs(seed: int = 0) -> dict:
    keys = jax.random.split(jax.random.key(seed), 11)
    return {
        "fields": draw_fields(jax.random.fold_in(keys[10], 71), 0),
        "cotangent": bell_draw(keys[1], (LEV, NLAT, NLON, C), 1.0, 6.0, ((1, 8), (2, 16))),
        "window_kinds": touch_ends(jax.random.randint(keys[2], (LEV // WZ, NLAT // WLAT), 0, TYPES), jax.random.fold_in(keys[2], 1), 0, TYPES - 1).astype(jnp.int32),
        "first_gain": jnp.clip(1.0 + 0.18 * jax.random.normal(keys[3], (C,), jnp.float32), 0.1, 1.9),
        "attend_weight": bell_draw(keys[4], (C, 3 * C), C ** -0.5, 0.4375),
        "output_weight": bell_draw(keys[5], (C, C), C ** -0.5, 0.4375),
        "second_gain": jnp.clip(1.0 + 0.18 * jax.random.normal(keys[6], (C,), jnp.float32), 0.1, 1.9),
        "expand_weight": bell_draw(keys[7], (C, HID), C ** -0.5, 0.4375),
        "shrink_weight": bell_draw(keys[8], (HID, C), HID ** -0.5, 0.21875),
        "bias_table": draw_bias_table(jax.random.fold_in(keys[10], 71), 0),
    }


eps = 1e-05

def window_offsets():
    level_pos, row_pos, column_pos = np.meshgrid(np.arange(WZ), np.arange(WLAT), np.arange(WLON), indexing='ij')
    level_pos = level_pos.reshape(-1)
    row_pos = row_pos.reshape(-1)
    column_pos = column_pos.reshape(-1)
    pair_level = level_pos[:, None] * WZ + level_pos[None, :]
    pair_row = row_pos[:, None] * WLAT + row_pos[None, :]
    relative = column_pos[:, None] - column_pos[None, :] + WLON - 1
    return ((pair_level * WLAT * WLAT + pair_row) * (2 * WLON - 1) + relative).reshape(-1).astype(np.int32)

def layer_norm(values, gain):
    center = values - lax.optimization_barrier(jnp.mean(values, axis=-1, keepdims=True))
    inverse = lax.rsqrt(lax.optimization_barrier(jnp.mean(center * center, axis=-1, keepdims=True)) + eps)
    scaled = center * inverse
    return (scaled * gain, scaled, inverse)

def norm_back(upstream, scaled, inverse, gain):
    weighted = upstream * gain
    return inverse * (weighted - lax.optimization_barrier(jnp.mean(weighted, axis=-1, keepdims=True)) - scaled * lax.optimization_barrier(jnp.mean(weighted * scaled, axis=-1, keepdims=True)))

def activation(values):
    normal_cdf = 0.5 * (1.0 + jax.scipy.special.erf(values * 0.7071067811865476))
    density = jnp.exp(-0.5 * values * values) * 0.3989422804014327
    return (values * normal_cdf, normal_cdf + values * density)

def window_grads(tokens, upstream, regions, window_kinds, first_gain, attend_weight, output_weight, second_gain, expand_weight, shrink_weight, bias_table):
    window_count, window_size, feature_width = tokens.shape
    head_count = bias_table.shape[1]
    type_count = bias_table.shape[0]
    head_width = feature_width // head_count
    row_total = window_count * window_size
    score_scale = head_width ** (-0.5)
    inputs = tokens.astype(jnp.float32).reshape(row_total, feature_width)
    normed_full, scaled_in, inverse_in = layer_norm(inputs, first_gain)
    normed_in = normed_full.astype(jnp.bfloat16)
    packed = jnp.dot(normed_in, attend_weight, preferred_element_type=jnp.float32).astype(jnp.bfloat16)
    packed = packed.reshape(window_count, window_size, 3, head_count, head_width)
    queries = packed[:, :, 0].astype(jnp.float32)
    key_heads = packed[:, :, 1].astype(jnp.float32)
    value_heads = packed[:, :, 2].astype(jnp.float32)
    offsets = jnp.asarray(window_offsets()).astype(jnp.int32)
    position_bias = jnp.take(bias_table[window_kinds], offsets, axis=2).reshape(window_count, head_count, window_size, window_size)
    allowed = (regions[:, :, None] == regions[:, None, :])[:, None]
    scores_raw = jnp.einsum('nqhd,nkhd->nhqk', queries, key_heads) * score_scale + position_bias
    scores_raw = jnp.where(allowed, scores_raw, -1e+30)
    largest = lax.optimization_barrier(jnp.max(scores_raw, axis=-1, keepdims=True))
    exponent = jnp.exp(scores_raw - largest)
    attention = exponent / lax.optimization_barrier(jnp.sum(exponent, axis=-1, keepdims=True))
    attention_low = attention.astype(jnp.bfloat16)
    mixed_heads = jnp.einsum('nhqk,nkhd->nqhd', attention_low.astype(jnp.float32), value_heads).astype(jnp.bfloat16).reshape(row_total, feature_width)
    residual = (inputs + jnp.dot(mixed_heads, output_weight, preferred_element_type=jnp.float32)).astype(jnp.bfloat16)
    normed_full, scaled_mid, inverse_mid = layer_norm(residual.astype(jnp.float32), second_gain)
    normed_mid = normed_full.astype(jnp.bfloat16)
    expanded = jnp.dot(normed_mid, expand_weight, preferred_element_type=jnp.float32)
    activated, gate_slope = activation(expanded)
    activated = activated.astype(jnp.bfloat16)
    upstream_flat = upstream.reshape(row_total, feature_width)
    grad_shrink = jnp.dot(activated.T, upstream_flat, preferred_element_type=jnp.float32)
    grad_expanded = (jnp.dot(upstream_flat, shrink_weight.T, preferred_element_type=jnp.float32) * gate_slope).astype(jnp.bfloat16)
    grad_expand = jnp.dot(normed_mid.T, grad_expanded, preferred_element_type=jnp.float32)
    grad_normed = jnp.dot(grad_expanded, expand_weight.T, preferred_element_type=jnp.float32)
    grad_second = lax.optimization_barrier(jnp.sum(grad_normed * scaled_mid, axis=0))
    grad_residual = norm_back(grad_normed, scaled_mid, inverse_mid, second_gain) + upstream_flat.astype(jnp.float32)
    grad_residual_low = grad_residual.astype(jnp.bfloat16)
    grad_output = jnp.dot(mixed_heads.T, grad_residual_low, preferred_element_type=jnp.float32)
    grad_mixed = jnp.dot(grad_residual_low, output_weight.T, preferred_element_type=jnp.float32).astype(jnp.bfloat16)
    grad_mixed = grad_mixed.reshape(window_count, window_size, head_count, head_width).astype(jnp.float32)
    grad_values = jnp.einsum('nhqk,nqhd->nkhd', attention_low.astype(jnp.float32), grad_mixed)
    grad_attention = jnp.einsum('nqhd,nkhd->nhqk', grad_mixed, value_heads)
    grad_scores = attention * (grad_attention - lax.optimization_barrier(jnp.sum(grad_attention * attention, axis=-1, keepdims=True)))
    per_position = jnp.zeros((window_count * head_count, POS), jnp.float32).at[:, offsets].add(grad_scores.reshape(window_count * head_count, window_size * window_size))
    choose_type = (window_kinds[:, None] == jnp.arange(type_count, dtype=jnp.int32)[None, :]).astype(jnp.float32)
    grad_table = jnp.einsum('nt,nhp->thp', choose_type, per_position.reshape(window_count, head_count, POS), precision=lax.Precision.HIGHEST)
    grad_scores_low = (grad_scores * score_scale).astype(jnp.bfloat16).astype(jnp.float32)
    grad_queries = jnp.einsum('nhqk,nkhd->nqhd', grad_scores_low, key_heads)
    grad_keys = jnp.einsum('nhqk,nqhd->nkhd', grad_scores_low, queries)
    grad_packed = jnp.stack([grad_queries, grad_keys, grad_values], axis=2).astype(jnp.bfloat16).reshape(row_total, 3 * feature_width)
    grad_attend = jnp.dot(normed_in.T, grad_packed, preferred_element_type=jnp.float32)
    grad_normed_in = jnp.dot(grad_packed, attend_weight.T, preferred_element_type=jnp.float32)
    grad_first = lax.optimization_barrier(jnp.sum(grad_normed_in * scaled_in, axis=0))
    grad_tokens = (norm_back(grad_normed_in, scaled_in, inverse_in, first_gain) + grad_residual).astype(jnp.bfloat16)
    return (grad_tokens.reshape(window_count, window_size, feature_width), (grad_first, grad_attend, grad_output, grad_second, grad_expand, grad_shrink, grad_table))

def to_windows(cell_grid):
    levels, row_count, column_count = cell_grid.shape[:3]
    trailing = cell_grid.shape[3:]
    blocked = cell_grid.reshape((levels // WZ, WZ, row_count // WLAT, WLAT, column_count // WLON, WLON) + trailing)
    axis_order = (2, 0, 4, 1, 3, 5) + tuple(range(6, 6 + len(trailing)))
    return blocked.transpose(axis_order).reshape((row_count // WLAT, levels // WZ * (column_count // WLON), WZ * WLAT * WLON) + trailing)

def from_windows(windows_in, levels, row_count, column_count):
    feature_width = windows_in.shape[-1]
    blocked = windows_in.reshape(row_count // WLAT, levels // WZ, column_count // WLON, WZ, WLAT, WLON, feature_width)
    return blocked.transpose(1, 3, 0, 4, 2, 5, 6).reshape(levels, row_count, column_count, feature_width)

def reference(fields, cotangent, window_kinds, first_gain, attend_weight, output_weight, second_gain, expand_weight, shrink_weight, bias_table):
    levels, row_count, column_count, feature_width = fields.shape
    hidden_width = expand_weight.shape[1]
    back_shift = (-(WZ // 2), -(WLAT // 2), -(WLON // 2))
    shifted_fields = jnp.roll(fields, back_shift, axis=(0, 1, 2))
    shifted_cotangent = jnp.roll(cotangent, back_shift, axis=(0, 1, 2))
    row_wrap = (jnp.arange(row_count, dtype=jnp.int32) >= row_count - WLAT // 2).astype(jnp.int32)
    level_wrap = (jnp.arange(levels, dtype=jnp.int32) >= levels - WZ // 2).astype(jnp.int32)
    region_grid = row_wrap[None, :] * 2 + level_wrap[:, None]
    region_cells = jnp.broadcast_to(region_grid[:, :, None], (levels, row_count, column_count))
    token_windows = to_windows(shifted_fields)
    upstream_windows = to_windows(shifted_cotangent)
    region_windows = to_windows(region_cells)
    kind_grid = jnp.broadcast_to(window_kinds.T[:, :, None], (row_count // WLAT, levels // WZ, column_count // WLON))
    kind_rows = kind_grid.reshape(row_count // WLAT, -1).astype(jnp.int32)
    initial = (jnp.zeros((feature_width,), jnp.float32), jnp.zeros((feature_width, 3 * feature_width), jnp.float32), jnp.zeros((feature_width, feature_width), jnp.float32), jnp.zeros((feature_width,), jnp.float32), jnp.zeros((feature_width, hidden_width), jnp.float32), jnp.zeros((hidden_width, feature_width), jnp.float32), jnp.zeros(bias_table.shape, jnp.float32))

    def scan_step(totals, pieces):
        grad_tokens, grads = window_grads(pieces[0], pieces[1], pieces[2], pieces[3], first_gain, attend_weight, output_weight, second_gain, expand_weight, shrink_weight, bias_table)
        return (jax.tree.map(jnp.add, totals, grads), grad_tokens)
    totals, grad_windows = lax.scan(scan_step, initial, (token_windows, upstream_windows, region_windows, kind_rows))
    norm_factor = 1.0 / math.sqrt(levels * row_count * column_count)
    grad_shifted = from_windows(grad_windows, levels, row_count, column_count)
    grad_fields = jnp.roll(grad_shifted, (WZ // 2, WLAT // 2, WLON // 2), axis=(0, 1, 2))
    return (grad_fields, totals[0] * norm_factor, totals[1] * norm_factor, totals[2] * norm_factor, totals[3] * norm_factor, totals[4] * norm_factor, totals[5] * norm_factor, totals[6])
```

```python
import functools
import math

import jax
import jax.numpy as jnp
import numpy as np
from jax import lax
from jax.experimental import pallas as pl
from jax.experimental.pallas import tpu as pltpu
from jax.sharding import PartitionSpec as P

F32, BF16 = jnp.float32, jnp.bfloat16
C, HEADS, HID = 192, 6, 768
WZ, WLAT, WLON = 2, 6, 12
LEV, ROWS, COLS = 4, 6, 24
POS, POSP = 3312, 3328
TYPES = 16
WIN = WZ * WLAT * WLON
ZA = WZ * WLAT
DIFFS = 2 * WLON - 1
LANES, LANESP = HEADS * WIN, 896
WIDE, WIDEP = DIFFS * HEADS * ZA, 1664
CODES, CODESP = DIFFS * ZA, 288
TOK = LEV * ROWS * COLS
HALF = TOK // 2
SCALE = (C // HEADS) ** (-0.5)
EPS = 1e-05


def constants():
    lane = np.arange(LANESP)
    lane_b, lane_h, lane_za = lane // 72, (lane // 12) % 6, lane % 12
    real = lane < LANES
    rep = ((lane_b * 12 + lane_za)[:, None] == np.arange(WIN)[None, :]) & real[:, None]
    heads = (lane_h[:, None] == (np.arange(C) // 32)[None, :]) & real[:, None]
    pos = np.arange(POSP)
    diff, rest = pos % DIFFS, pos // DIFFS
    aq, ap, zq, zp = rest % 6, rest // 6 % 6, rest // 36 % 2, rest // 72
    fine = pos < POS
    code = np.where(fine, diff * ZA + zp * 6 + ap, -1)
    rho = np.where(fine, zq * 6 + aq, -1)
    pos_codes = np.stack([code, rho]).astype(np.int32)
    wide = np.arange(WIDEP)
    wide_r, wide_h, wide_za = wide // 72, (wide // 12) % 6, wide % 12
    okay = wide < WIDE
    spread = ((wide_r * 12 + wide_za)[None, :] == np.arange(CODESP)[:, None]) & okay[None, :]
    wide_codes = np.stack(
        [np.where(okay, wide_h, -1), wide_za // 6, (wide_za % 6) // 3]
    ).astype(np.int32)
    out_row = np.arange(HALF)
    lon, za = out_row // ZA, out_row % ZA
    order = np.arange(HALF)[None, :] == (za * COLS + lon)[:, None]
    low = lambda a: jnp.asarray(a.astype(np.float32), BF16)
    return (
        low(rep), low(rep.T), low(heads), low(heads.T),
        jnp.asarray(pos_codes), jnp.asarray(wide_codes), low(spread), low(spread.T), low(order), low(order.T),
    )


def dot(a, b, dims=((1,), (0,))):
    return lax.dot_general(a, b, (dims, ((), ())), preferred_element_type=F32)


NT = ((1,), (1,))
TN = ((0,), (0,))


def split3(v):
    hi = v.astype(BF16)
    rest = v - hi.astype(F32)
    mid = rest.astype(BF16)
    lo = (rest - mid.astype(F32)).astype(BF16)
    return hi, mid, lo


def norm(values):
    center = values - jnp.mean(values, axis=-1, keepdims=True)
    inverse = lax.rsqrt(jnp.mean(center * center, axis=-1, keepdims=True) + EPS)
    return center * inverse, inverse


def norm_back(weighted, scaled, inverse):
    return inverse * (
        weighted
        - jnp.mean(weighted, axis=-1, keepdims=True)
        - scaled * jnp.mean(weighted * scaled, axis=-1, keepdims=True)
    )


def activation(values):
    normal_cdf = 0.5 * (1.0 + lax.erf(values * 0.7071067811865476))
    density = jnp.exp(-0.5 * values * values) * 0.3989422804014327
    return values * normal_cdf, normal_cdf + values * density


def prepare_bias(lat, kinds, table, pos_codes, wide_codes, spread, tsel, tmask, wt, wall, onehot, bias):
    code = pos_codes[0:1, :]
    rho = pos_codes[1:2, :]
    for row in range(0, CODESP, 16):
        rows = lax.broadcasted_iota(jnp.int32, (16, POSP), 0) + row
        onehot[row : row + 16, :] = jnp.where(rows == code, 1.0, 0.0).astype(BF16)
    tsel[...] = jnp.zeros_like(tsel)
    kind_rows = lax.broadcasted_iota(jnp.int32, (TYPES, POS), 0)
    for i in range(2):
        pick = kind_rows == kinds[i, 0]
        for h in range(HEADS):
            chosen = jnp.sum(jnp.where(pick, table[h], 0.0), axis=0, keepdims=True)
            tsel[i * HEADS + h : i * HEADS + h + 1, :POS] = chosen
    mine = lax.broadcasted_iota(jnp.int32, (ZA, POSP), 0) == rho
    total = None
    for part in range(3):
        if part:
            tsel[...] = tsel[...] - tsel[...].astype(BF16).astype(F32)
        for k in range(2 * HEADS):
            tmask[k * ZA : (k + 1) * ZA, :] = jnp.where(mine, tsel[k : k + 1, :], 0.0)
        piece = dot(tmask[...].astype(BF16), onehot[...], NT)
        total = piece if total is None else total + piece
    spreaded = None
    for piece in split3(total):
        term = dot(piece, spread[...])
        spreaded = term if spreaded is None else spreaded + term
    wt[...] = spreaded
    own_head = wide_codes[0:1, :]
    row_id = lax.broadcasted_iota(jnp.int32, (ZA, WIDEP), 0)
    row_z = (row_id >= 6).astype(jnp.int32)
    row_a = row_id - 6 * row_z
    level_cut = row_z != wide_codes[1:2, :]
    row_cut = (row_a >= 3).astype(jnp.int32) != wide_codes[2:3, :]
    last = jnp.full((ZA, WIDEP), lat, jnp.int32) == lax.axis_size("lat") - 1
    bias[...] = jnp.zeros_like(bias)
    for i in range(2):
        acc = jnp.zeros((ZA, WIDEP), F32)
        for h in range(HEADS):
            start = (i * HEADS + h) * ZA
            acc = acc + jnp.where(own_head == h, wt[start : start + ZA, :], 0.0)
        cut = row_cut & last
        if i == 1:
            cut = cut | level_cut
        wall[i, 0:ZA, :] = jnp.where(cut, -1e30, acc)
        for b in range(WLON):
            start = (WLON - 1 - b) * 72
            bias[i, b * ZA : (b + 1) * ZA, 0:LANES] = wall[i, 0:ZA, start : start + LANES]


def compute(
    kinds, x_in, c_in, g1, wa, wo, g2, we, ws, table,
    rep, rep_t, heads, heads_t, pos_codes, wide_codes, spread, spread_t, order, order_t,
    gx, gains, d_attend, d_output, d_expand, d_shrink, per_pos,
    tsel, tmask, wt, wall, onehot, bias,
    xs, cs, scaled_in, inv_in, normed_in, packed, q_stack, scores, attn, attn_low, mixed,
    scaled_mid, inv_mid, normed_mid, big, big2, act, gexp, gres, gmix, m_stack, grad_scores, scores_low,
    gpack, gacc, gconv,
):
    lat = lax.axis_index("lat")
    prepare_bias(lat, kinds, table, pos_codes, wide_codes, spread, tsel, tmask, wt, wall, onehot, bias)
    for i in range(2):
        rows = slice(i * HALF, (i + 1) * HALF)
        xs[rows, :] = dot(order[...], x_in[rows, :])
        cs[rows, :] = dot(order[...], c_in[rows, :]).astype(BF16)
    step = 96
    for start in range(0, TOK, step):
        rows = slice(start, start + step)
        scaled, inverse = norm(xs[rows, :])
        scaled_in[rows, :] = scaled
        inv_in[rows, :] = inverse
        normed_in[rows, :] = (scaled * g1[...]).astype(BF16)
    for part in range(3):
        weight = wa[:, part * C : (part + 1) * C]
        packed[part] = dot(normed_in[...], weight).astype(BF16)
    for w in range(4):
        rows = slice(w * WIN, (w + 1) * WIN)
        i = w // 2
        query, key, value = packed[0, rows, :], packed[1, rows, :], packed[2, rows, :]
        q_stack[w] = dot(rep[...], query).astype(BF16) * heads[...]
        scores[...] = dot(key, q_stack[w], NT)
        for lane in range(0, LANESP, 128):
            lanes = slice(lane, lane + 128)
            s = scores[:, lanes] * SCALE + bias[i, :, lanes]
            e = jnp.exp(s - jnp.max(s, axis=0, keepdims=True))
            a = e * (1.0 / jnp.sum(e, axis=0, keepdims=True))
            attn[w, :, lanes] = a
            attn_low[w, :, lanes] = a.astype(BF16)
        value_t = value.astype(F32).T.astype(BF16)
        per_head = dot(value_t, attn_low[w]).astype(BF16) * heads_t[...]
        mixed[rows, :] = dot(rep_t[...], per_head, NT).astype(BF16)
    big2[:, 0:C] = dot(mixed[...], wo[...])
    for start in range(0, TOK, step):
        rows = slice(start, start + step)
        residual = (xs[rows, :] + big2[rows, 0:C]).astype(BF16).astype(F32)
        scaled, inverse = norm(residual)
        scaled_mid[rows, :] = scaled
        inv_mid[rows, :] = inverse
        normed_mid[rows, :] = (scaled * g2[...]).astype(BF16)
    big[...] = dot(normed_mid[...], we[...])
    big2[...] = dot(cs[...], ws[...])
    for start in range(0, TOK, 16):
        rows = slice(start, start + 16)
        activated, slope = activation(big[rows, :])
        act[rows, :] = activated.astype(BF16)
        gexp[rows, :] = (big2[rows, :] * slope).astype(BF16)
    d_shrink[...] = dot(cs[...], act[...], TN)
    d_expand[...] = dot(normed_mid[...], gexp[...], TN)
    big[:, 0:C] = dot(gexp[...], we[...], NT)
    gain_sum = jnp.zeros((1, C), F32)
    for start in range(0, TOK, step):
        rows = slice(start, start + step)
        grad = big[rows, 0:C]
        scaled = scaled_mid[rows, :]
        gain_sum = gain_sum + jnp.sum(grad * scaled, axis=0, keepdims=True)
        gres[rows, :] = norm_back(grad * g2[...], scaled, inv_mid[rows, :]) + cs[rows, :].astype(F32)
    gains[1:2, :] = gain_sum
    grad_low = gres[...].astype(BF16)
    d_output[...] = dot(mixed[...], grad_low, TN)
    gmix[...] = dot(grad_low, wo[...], NT).astype(BF16)
    for w in range(4):
        rows = slice(w * WIN, (w + 1) * WIN)
        i = w // 2
        key, value = packed[1, rows, :], packed[2, rows, :]
        m_stack[...] = dot(rep[...], gmix[rows, :]).astype(BF16) * heads[...]
        gpack[2, rows, :] = dot(attn_low[w], m_stack[...]).astype(BF16)
        scores[...] = dot(value, m_stack[...], NT)
        for lane in range(0, LANESP, 128):
            lanes = slice(lane, lane + 128)
            a = attn[w, :, lanes]
            da = scores[:, lanes]
            ds = a * (da - jnp.sum(da * a, axis=0, keepdims=True))
            scores_low[:, lanes] = (ds * SCALE).astype(BF16)
            if w % 2 == 0:
                grad_scores[:, lanes] = ds
            else:
                grad_scores[:, lanes] = grad_scores[:, lanes] + ds
        gpack[1, rows, :] = dot(scores_low[...], q_stack[w]).astype(BF16)
        key_t = key.astype(F32).T.astype(BF16)
        per_head = dot(key_t, scores_low[...]).astype(BF16) * heads_t[...]
        gpack[0, rows, :] = dot(rep_t[...], per_head, NT).astype(BF16)
        if w % 2 == 1:
            gacc[...] = jnp.zeros_like(gacc)
            for b in range(WLON):
                start = (WLON - 1 - b) * 72
                gacc[0:ZA, start : start + LANES] = (
                    gacc[0:ZA, start : start + LANES] + grad_scores[b * ZA : (b + 1) * ZA, 0:LANES]
                )
            own_head = wide_codes[0:1, :]
            for h in range(HEADS):
                place = (i * HEADS + h) * ZA
                wt[place : place + ZA, :] = jnp.where(own_head == h, gacc[0:ZA, :], 0.0)
    folded = dot(wt[...].astype(BF16), spread_t[...]).astype(BF16)
    tmask[...] = dot(folded, onehot[...])
    mine = lax.broadcasted_iota(jnp.int32, (ZA, POSP), 0) == pos_codes[1:2, :]
    for k in range(2 * HEADS):
        per_pos[k : k + 1, :] = jnp.sum(
            jnp.where(mine, tmask[k * ZA : (k + 1) * ZA, :], 0.0), axis=0, keepdims=True
        )
    back = None
    for part in range(3):
        lanes = slice(part * C, (part + 1) * C)
        d_attend[:, lanes] = dot(normed_in[...], gpack[part], TN)
        term = dot(gpack[part], wa[:, lanes], NT)
        back = term if back is None else back + term
    big[:, 0:C] = back
    gain_sum = jnp.zeros((1, C), F32)
    for start in range(0, TOK, step):
        rows = slice(start, start + step)
        grad = big[rows, 0:C]
        scaled = scaled_in[rows, :]
        gain_sum = gain_sum + jnp.sum(grad * scaled, axis=0, keepdims=True)
        result = norm_back(grad * g1[...], scaled, inv_in[rows, :]) + gres[rows, :]
        act[rows, 0:C] = result.astype(BF16)
    gains[0:1, :] = gain_sum
    for i in range(2):
        rows = slice(i * HALF, (i + 1) * HALF)
        gx[rows, :] = dot(order_t[...], act[rows, 0:C]).astype(BF16)


def local_scratch():
    return [
        pltpu.VMEM((16, POSP), F32),
        pltpu.VMEM((WIN, POSP), F32),
        pltpu.VMEM((WIN, WIDEP), F32),
        pltpu.VMEM((2, 16, WIDEP), F32),
        pltpu.VMEM((CODESP, POSP), BF16),
        pltpu.VMEM((2, WIN, LANESP), F32),
        pltpu.VMEM((TOK, C), F32),
        pltpu.VMEM((TOK, C), BF16),
        pltpu.VMEM((TOK, C), F32),
        pltpu.VMEM((TOK, 1), F32),
        pltpu.VMEM((TOK, C), BF16),
        pltpu.VMEM((3, TOK, C), BF16),
        pltpu.VMEM((4, LANESP, C), BF16),
        pltpu.VMEM((WIN, LANESP), F32),
        pltpu.VMEM((4, WIN, LANESP), F32),
        pltpu.VMEM((4, WIN, LANESP), BF16),
        pltpu.VMEM((TOK, C), BF16),
        pltpu.VMEM((TOK, C), F32),
        pltpu.VMEM((TOK, 1), F32),
        pltpu.VMEM((TOK, C), BF16),
        pltpu.VMEM((TOK, HID), F32),
        pltpu.VMEM((TOK, HID), F32),
        pltpu.VMEM((TOK, HID), BF16),
        pltpu.VMEM((TOK, HID), BF16),
        pltpu.VMEM((TOK, C), F32),
        pltpu.VMEM((TOK, C), BF16),
        pltpu.VMEM((LANESP, C), BF16),
        pltpu.VMEM((WIN, LANESP), F32),
        pltpu.VMEM((WIN, LANESP), BF16),
        pltpu.VMEM((3, TOK, C), BF16),
        pltpu.VMEM((16, WIDEP), F32),
        pltpu.VMEM((16, 128), F32),
    ]


def local_call(kinds, x, c, g1, wa, wo, g2, we, ws_t, table_h):
    shapes = [
        ((TOK, C), BF16), ((2, C), F32), ((C, 3 * C), F32), ((C, C), F32),
        ((C, HID), F32), ((C, HID), F32), ((2 * HEADS, POSP), F32),
    ]
    vm = pl.BlockSpec(memory_space=pltpu.VMEM)
    return pl.pallas_call(
        compute,
        out_shape=[jax.ShapeDtypeStruct(s, d) for s, d in shapes],
        in_specs=[pl.BlockSpec(memory_space=pltpu.SMEM)] + [vm] * 19,
        out_specs=[vm] * 7,
        scratch_shapes=local_scratch(),
        compiler_params=pltpu.CompilerParams(vmem_limit_bytes=60 * 2**20),
        name="block_backward",
    )(kinds, x, c, g1[None], wa, wo, g2[None], we, ws_t, table_h, *constants())

def shifted(array, axis, by):
    size = lax.axis_size(axis)
    return lax.ppermute(array, axis, [(i, (i + by) % size) for i in range(size)])


def body(
    fields, cotangent, window_kinds, first_gain, attend_weight, output_weight,
    second_gain, expand_weight, shrink_weight, bias_table,
):
    stacked = jnp.stack([fields, cotangent])
    arrived = shifted(stacked[:, :, :, :6], "lon", -1)
    stacked = jnp.concatenate([stacked[:, :, :, 6:], arrived], axis=3)
    arrived = shifted(stacked[:, :, :3], "lat", -1)
    stacked = jnp.concatenate([stacked[:, :, 3:], arrived], axis=2)
    stacked = jnp.concatenate([stacked[:, 1:], stacked[:, :1]], axis=1).reshape(2, TOK, C)
    gx, gains, d_attend, d_output, d_expand, d_shrink, per_pos = local_call(
        window_kinds, stacked[0], stacked[1], first_gain, attend_weight, output_weight,
        second_gain, expand_weight, shrink_weight.T, bias_table.transpose(1, 0, 2),
    )
    flat = jnp.concatenate([d_attend, d_output, d_expand, d_shrink], axis=1)
    gains, flat = lax.psum((gains, flat), ("lon", "lat"))
    per_pos = lax.psum(per_pos, "lon")
    per_pos = lax.all_gather(per_pos, "lat").reshape(-1, 2, HEADS, POSP)[..., :POS]
    all_kinds = lax.all_gather(window_kinds[:, 0], "lat")
    choose = (all_kinds[:, :, None] == jnp.arange(TYPES)[None, None, :]).astype(F32)
    table = jnp.einsum("jit,jihp->htp", choose, per_pos, precision=lax.Precision.HIGHEST)
    cell = gx.reshape(LEV, ROWS, COLS, C)
    cell = jnp.concatenate([cell[3:], cell[:3]], axis=0)
    cell = jnp.concatenate([shifted(cell[:, :, 18:], "lon", 1), cell[:, :, :18]], axis=2)
    cell = jnp.concatenate([shifted(cell[:, 3:], "lat", 1), cell[:, :3]], axis=1)
    f = 1.0 / math.sqrt(TOK * lax.axis_size("lon") * lax.axis_size("lat"))
    return (
        cell, gains[0] * f, flat[:, :576] * f, flat[:, 576:768] * f, gains[1] * f,
        flat[:, 768:1536] * f, flat[:, 1536:].T * f, table.transpose(1, 0, 2),
    )


def solution(mesh):
    cells = P(None, "lat", "lon", None)
    in_specs = (cells, cells, P(None, "lat")) + (P(),) * 7
    out_specs = (cells,) + (P(),) * 7
    return jax.shard_map(body, mesh=mesh, in_specs=in_specs, out_specs=out_specs, check_vma=False)
```

```python
import functools
import math

import jax
import jax.numpy as jnp
import numpy as np
from jax import lax
from jax.experimental import pallas as pl
from jax.experimental.pallas import tpu as pltpu
from jax.sharding import PartitionSpec as P

F32, BF16 = jnp.float32, jnp.bfloat16
C, HEADS, HID = 192, 6, 768
WZ, WLAT, WLON = 2, 6, 12
LEV, ROWS, COLS = 4, 6, 24
POS, POSP = 3312, 3328
TYPES = 16
WIN = WZ * WLAT * WLON
ZA = WZ * WLAT
DIFFS = 2 * WLON - 1
LANES, LANESP = HEADS * WIN, 896
WIDE, WIDEP = DIFFS * HEADS * ZA, 1664
CODES, CODESP = DIFFS * ZA, 288
TOK = LEV * ROWS * COLS
HALF = TOK // 2
SCALE = (C // HEADS) ** (-0.5)
EPS = 1e-05


def constants():
    lane = np.arange(LANESP)
    lane_b, lane_h, lane_za = lane // 72, (lane // 12) % 6, lane % 12
    real = lane < LANES
    rep = ((lane_b * 12 + lane_za)[:, None] == np.arange(WIN)[None, :]) & real[:, None]
    heads = (lane_h[:, None] == (np.arange(C) // 32)[None, :]) & real[:, None]
    pos = np.arange(POSP)
    diff, rest = pos % DIFFS, pos // DIFFS
    aq, ap, zq, zp = rest % 6, rest // 6 % 6, rest // 36 % 2, rest // 72
    fine = pos < POS
    code = np.where(fine, diff * ZA + zp * 6 + ap, -1)
    rho = np.where(fine, zq * 6 + aq, -1)
    pos_codes = np.stack([code, rho]).astype(np.int32)
    wide = np.arange(WIDEP)
    wide_r, wide_h, wide_za = wide // 72, (wide // 12) % 6, wide % 12
    okay = wide < WIDE
    spread = ((wide_r * 12 + wide_za)[None, :] == np.arange(CODESP)[:, None]) & okay[None, :]
    wide_codes = np.stack(
        [np.where(okay, wide_h, -1), wide_za // 6, (wide_za % 6) // 3]
    ).astype(np.int32)
    cell = np.arange(HALF)
    lon, z, a = cell // ZA, cell % ZA // 6, cell % 6
    place = np.where(
        a < 3,
        np.where(lon < 18, (z * 3 + a) * 18 + lon, 112 + (z * 3 + a) * 6 + lon - 18),
        np.where(lon < 18, 160 + (z * 3 + a - 3) * 18 + lon, 272 + (z * 3 + a - 3) * 6 + lon - 18),
    )
    order = place[:, None] == np.arange(320)[None, :]
    z, a, lon = cell // 144, cell % 144 // 24, cell % 24
    place = np.where(
        a >= 3,
        np.where(lon >= 6, (z * 3 + a - 3) * 18 + lon - 6, 112 + (z * 3 + a - 3) * 6 + lon),
        np.where(lon >= 6, 160 + (z * 3 + a) * 18 + lon - 6, 272 + (z * 3 + a) * 6 + lon),
    )
    grid = np.arange(320)[:, None] == place[None, :]
    low = lambda a: jnp.asarray(a.astype(np.float32), BF16)
    return (
        low(rep), low(rep.T), low(heads), low(heads.T),
        jnp.asarray(pos_codes), jnp.asarray(wide_codes), low(spread), low(spread.T), low(order), low(order.T), low(grid),
    )


def dot(a, b, dims=((1,), (0,))):
    return lax.dot_general(a, b, (dims, ((), ())), preferred_element_type=F32)


NT = ((1,), (1,))
TN = ((0,), (0,))


def split3(v):
    hi = v.astype(BF16)
    rest = v - hi.astype(F32)
    mid = rest.astype(BF16)
    lo = (rest - mid.astype(F32)).astype(BF16)
    return hi, mid, lo


def norm(values):
    center = values - jnp.mean(values, axis=-1, keepdims=True)
    inverse = lax.rsqrt(jnp.mean(center * center, axis=-1, keepdims=True) + EPS)
    return center * inverse, inverse


def norm_back(weighted, scaled, inverse):
    return inverse * (
        weighted
        - jnp.mean(weighted, axis=-1, keepdims=True)
        - scaled * jnp.mean(weighted * scaled, axis=-1, keepdims=True)
    )


def activation(values):
    normal_cdf = 0.5 * (1.0 + lax.erf(values * 0.7071067811865476))
    density = jnp.exp(-0.5 * values * values) * 0.3989422804014327
    return values * normal_cdf, normal_cdf + values * density


def prepare_bias(lat, kinds, table, pos_codes, wide_codes, spread, tsel, tmask, wt, wall, onehot, bias):
    code = pos_codes[0:1, :]
    rho = pos_codes[1:2, :]
    for row in range(0, CODESP, 16):
        rows = lax.broadcasted_iota(jnp.int32, (16, POSP), 0) + row
        onehot[row : row + 16, :] = jnp.where(rows == code, 1.0, 0.0).astype(BF16)
    tsel[...] = jnp.zeros_like(tsel)
    kind_rows = lax.broadcasted_iota(jnp.int32, (TYPES, POS), 0)
    for i in range(2):
        pick = kind_rows == kinds[i, 0]
        for h in range(HEADS):
            chosen = jnp.sum(jnp.where(pick, table[h], 0.0), axis=0, keepdims=True)
            tsel[i * HEADS + h : i * HEADS + h + 1, :POS] = chosen
    mine = lax.broadcasted_iota(jnp.int32, (ZA, POSP), 0) == rho
    total = None
    for part in range(3):
        if part:
            tsel[...] = tsel[...] - tsel[...].astype(BF16).astype(F32)
        for k in range(2 * HEADS):
            tmask[k * ZA : (k + 1) * ZA, :] = jnp.where(mine, tsel[k : k + 1, :], 0.0)
        piece = dot(tmask[...].astype(BF16), onehot[...], NT)
        total = piece if total is None else total + piece
    spreaded = None
    for piece in split3(total):
        term = dot(piece, spread[...])
        spreaded = term if spreaded is None else spreaded + term
    wt[...] = spreaded
    own_head = wide_codes[0:1, :]
    row_id = lax.broadcasted_iota(jnp.int32, (ZA, WIDEP), 0)
    row_z = (row_id >= 6).astype(jnp.int32)
    row_a = row_id - 6 * row_z
    level_cut = row_z != wide_codes[1:2, :]
    row_cut = (row_a >= 3).astype(jnp.int32) != wide_codes[2:3, :]
    last = jnp.full((ZA, WIDEP), lat, jnp.int32) == lax.axis_size("lat") - 1
    bias[...] = jnp.zeros_like(bias)
    for i in range(2):
        acc = jnp.zeros((ZA, WIDEP), F32)
        for h in range(HEADS):
            start = (i * HEADS + h) * ZA
            acc = acc + jnp.where(own_head == h, wt[start : start + ZA, :], 0.0)
        cut = row_cut & last
        if i == 1:
            cut = cut | level_cut
        wall[i, 0:ZA, :] = jnp.where(cut, -1e30, acc)
        for b in range(WLON):
            start = (WLON - 1 - b) * 72
            bias[i, b * ZA : (b + 1) * ZA, 0:LANES] = wall[i, 0:ZA, start : start + LANES]


MESH = pl.DeviceIdType.MESH


class Place:
    def __init__(self):
        self.lon, self.lat = lax.axis_index("lon"), lax.axis_index("lat")
        self.core = lax.rem(self.lon, 2)
        self.ring = lax.div(self.lon, 2)

    def twin(self):
        return (self.lon + 1 - 2 * self.core, self.lat)

    def ring_at(self, k):
        return lax.rem(self.ring + k, 8)

    def ring_peer(self, k):
        return (self.ring_at(k) * 2 + self.core, self.lat)

    def lat_peer(self, k):
        return (self.lon, lax.rem(self.lat + k, 8))

    def beside(self, east, north):
        return (lax.rem(self.lon + 16 + east, 16), lax.rem(self.lat + 8 + north, 8))


def greet(me):
    others = [me.twin()]
    others += [me.ring_peer(k) for k in range(1, 8)] + [me.lat_peer(k) for k in range(1, 8)]
    others += [me.beside(1, 0), me.beside(-1, 0), me.beside(1, 1), me.beside(-1, -1)]
    barrier = pltpu.get_barrier_semaphore()
    for other in others:
        pl.semaphore_signal(barrier, inc=1, device_id=other, device_id_type=MESH)
    return lambda: pl.semaphore_wait(barrier, len(others))


def remote(src, dst, sems, index, device):
    return pltpu.make_async_remote_copy(
        src_ref=src, dst_ref=dst, send_sem=sems.at[0, index], recv_sem=sems.at[1, index],
        device_id=device, device_id_type=MESH,
    )


class Edges:
    def __init__(self, me, src, dst, sems, base, by):
        pieces = ((224, 320, (by, 0)), (320, 544, (0, by)), (544, 640, (by, by)))
        self.copies = [
            remote(src.at[pl.ds(lo, hi - lo)], dst.at[pl.ds(lo, hi - lo)], sems, base + j, me.beside(*way))
            for j, (lo, hi, way) in enumerate(pieces)
        ]

    def start(self):
        for copy in self.copies:
            copy.start()

    def finish(self):
        for copy in self.copies:
            copy.wait()


EDGE_PARTS = ((0, 112, 0), (112, 160, 224), (160, 272, 320), (272, 320, 544))


def spread_pieces(dst, pieces, i):
    for lo, hi, base in EDGE_PARTS:
        n = hi - lo
        dst[base + i * n : base + (i + 1) * n, :] = pieces[lo:hi, :]


def gathered_pieces(src, i):
    return jnp.concatenate(
        [src[base + i * (hi - lo) : base + (i + 1) * (hi - lo), :] for lo, hi, base in EDGE_PARTS], axis=0
    )


def span(ref, start, n):
    return ref.at[pl.ds(pl.multiple_of(start, 16), n)]


class Summed:
    def __init__(self, me, sems, base, n, pay, arrived, first, second, full):
        self.me, self.sems, self.base, self.n = me, sems, base, n
        self.pay, self.arrived, self.first, self.second, self.full = pay, arrived, first, second, full

    def core_start(self):
        n = self.n
        self.core_copy = remote(
            span(self.pay, (1 - self.me.core) * 8 * n, 8 * n), self.arrived, self.sems, self.base, self.me.twin()
        )
        self.core_copy.start()

    def core_finish(self):
        self.core_copy.wait()
        n = self.n
        for s in range(8):
            place = pl.ds(pl.multiple_of(self.me.core * 8 * n + s * n, 16), n)
            mine = self.pay[place, :].astype(F32) + self.arrived[s * n : (s + 1) * n, :].astype(F32)
            self.pay[place, :] = mine.astype(BF16)

    def scatter_start(self):
        me, n = self.me, self.n
        self.scatter = [
            remote(
                span(self.pay, (me.core * 8 + me.ring_at(k)) * n, n), self.first.at[k - 1],
                self.sems, self.base + k, me.ring_peer(k),
            )
            for k in range(1, 8)
        ]
        for copy in self.scatter:
            copy.start()

    def scatter_finish(self):
        me, n = self.me, self.n
        total = self.pay[pl.ds(pl.multiple_of((me.core * 8 + me.ring) * n, 16), n), :].astype(F32)
        for copy in self.scatter:
            copy.wait_recv()
        for k in range(7):
            total = total + self.first[k].astype(F32)
        self.second[me.lat] = total.astype(BF16)

    def exchange_start(self):
        me = self.me
        self.exchange = [
            remote(self.second.at[me.lat], self.second.at[me.lat], self.sems, self.base + 7 + k, me.lat_peer(k))
            for k in range(1, 8)
        ]
        for copy in self.exchange:
            copy.start()

    def exchange_finish(self):
        for copy in self.exchange:
            copy.wait_recv()
        total = self.second[0].astype(F32)
        for k in range(1, 8):
            total = total + self.second[k].astype(F32)
        me, n = self.me, self.n
        self.full[pl.ds(pl.multiple_of((me.core * 8 + me.ring) * n, 16), n), :] = total.astype(BF16)

    def gather_start(self):
        me, n = self.me, self.n
        own = span(self.full, (me.core * 8 + me.ring) * n, n)
        self.gather = [
            remote(own, own, self.sems, self.base + 14 + k, me.ring_peer(k)) for k in range(1, 8)
        ]
        for copy in self.gather:
            copy.start()

    def gather_finish(self):
        for copy in self.gather:
            copy.wait_recv()

    def back_start(self):
        half = span(self.full, self.me.core * 8 * self.n, 8 * self.n)
        self.back = remote(half, half, self.sems, self.base + 22, self.me.twin())
        self.back.start()

    def back_finish(self):
        self.back.wait()
        for copy in self.scatter + self.exchange + self.gather:
            copy.wait_send()


class Tables(Summed):
    def core_start(self):
        self.core_copy = remote(self.pay, self.arrived, self.sems, self.base, self.me.twin())
        self.core_copy.start()

    def core_finish(self):
        self.core_copy.wait()
        self.pay[...] = (self.pay[...].astype(F32) + self.arrived[...].astype(F32)).astype(BF16)

    def scatter_start(self):
        me, n = self.me, self.n
        self.scatter = [
            remote(
                span(self.pay, me.ring_at(k) * n, n), self.first.at[k - 1],
                self.sems, self.base + k, me.ring_peer(k),
            )
            for k in range(1, 8)
        ]
        for copy in self.scatter:
            copy.start()

    def own(self):
        me = self.me
        return ((me.core * 8 + me.ring) * 4 + lax.div(me.lat, 2)) * self.n

    def scatter_finish(self):
        me, n = self.me, self.n
        total = self.pay[pl.ds(pl.multiple_of(me.ring * n, 16), n), :].astype(F32)
        for copy in self.scatter:
            copy.wait_recv()
        for k in range(7):
            total = total + self.first[k].astype(F32)
        self.second[...] = total.astype(BF16)

    def exchange_start(self):
        me = self.me
        self.mine = lax.rem(me.lat, 2) == me.core
        place = span(self.full, self.own(), self.n)
        self.exchange = [
            remote(self.second, place, self.sems, self.base + 7 + k, me.lat_peer(k)) for k in range(1, 8)
        ]

        @pl.when(self.mine)
        def _():
            self.full[pl.ds(pl.multiple_of(self.own(), 16), self.n), :] = self.second[...]
            for copy in self.exchange:
                copy.start()

    def exchange_finish(self):
        @pl.when(self.mine)
        def _():
            for copy in self.exchange[1::2]:
                copy.wait_recv()
            for copy in self.exchange:
                copy.wait_send()

        @pl.when(jnp.logical_not(self.mine))
        def _():
            for copy in self.exchange[0::2]:
                copy.wait_recv()

    def gather_start(self):
        me, n = self.me, self.n
        own = span(self.full, (me.core * 8 + me.ring) * 4 * n, 4 * n)
        self.gather = [
            remote(own, own, self.sems, self.base + 14 + k, me.ring_peer(k)) for k in range(1, 8)
        ]
        for copy in self.gather:
            copy.start()

    def back_start(self):
        half = span(self.full, self.me.core * 32 * self.n, 32 * self.n)
        self.back = remote(half, half, self.sems, self.base + 22, self.me.twin())
        self.back.start()

    def back_finish(self):
        self.back.wait()
        for copy in self.scatter + self.gather:
            copy.wait_send()


def block(
    kinds, x_in, c_in, g1, wa, wo, g2, we, ws, table,
    rep, rep_t, heads, heads_t, pos_codes, wide_codes, spread, spread_t, order, order_t, grid,
    edge_hbm, m_hbm, t_hbm, b_hbm,
    tsel, tmask, wt, wall, onehot, bias,
    xs, cs, scaled_in, inv_in, normed_in, packed, q_stack, scores, attn, attn_low, mixed,
    scaled_mid, inv_mid, normed_mid, big, big2, act, gexp, gres, gmix, m_stack, grad_scores, scores_low,
    gpack, gacc, gconv, gains, d_wide,
    x_out, c_out, push_out, x_got, c_got, edge_out,
    m_pay, m_arrived, m_first, m_second, m_full,
    t_pay, t_arrived, t_first, t_second, t_full,
    b_pay, b_arrived, b_first, b_second, b_full,
    sems, local,
):
    me = Place()
    wait_all = greet(me)
    m_sum = Summed(me, sems, 9, 144, m_pay, m_arrived, m_first, m_second, m_full)
    t_sum = Summed(me, sems, 32, 80, t_pay, t_arrived, t_first, t_second, t_full)
    b_sum = Tables(me, sems, 55, 48, b_pay, b_arrived, b_first, b_second, b_full)
    gains[...] = jnp.zeros_like(gains)
    edges = []
    for src, out, got, base in ((x_in, x_out, x_got, 0), (c_in, c_out, c_got, 3)):
        spread_pieces(out, dot(grid[...], src[144:432, :]).astype(BF16), 0)
        ends = jnp.concatenate([src[432:576, :], src[0:144, :]], axis=0)
        spread_pieces(out, dot(grid[...], ends).astype(BF16), 1)
        edges.append(Edges(me, out, got, sems, base, -1))
    wait_all()
    for edge in edges:
        edge.start()
    x_got[0:224, :] = x_out[0:224, :]
    c_got[0:224, :] = c_out[0:224, :]
    prepare_bias(me.lat, kinds, table, pos_codes, wide_codes, spread, tsel, tmask, wt, wall, onehot, bias)
    edges[0].finish()
    for i in range(2):
        xs[i * HALF : (i + 1) * HALF, :] = dot(order[...], gathered_pieces(x_got, i))
    step = 96
    for start in range(0, TOK, step):
        rows = slice(start, start + step)
        scaled, inverse = norm(xs[rows, :])
        scaled_in[rows, :] = scaled
        inv_in[rows, :] = inverse
        normed_in[rows, :] = (scaled * g1[...]).astype(BF16)
    for part in range(3):
        weight = wa[:, part * C : (part + 1) * C]
        packed[part] = dot(normed_in[...], weight).astype(BF16)
    for w in range(4):
        rows = slice(w * WIN, (w + 1) * WIN)
        i = w // 2
        query, key, value = packed[0, rows, :], packed[1, rows, :], packed[2, rows, :]
        q_stack[w] = dot(rep[...], query).astype(BF16) * heads[...]
        scores[...] = dot(key, q_stack[w], NT)
        for lane in range(0, LANESP, 128):
            lanes = slice(lane, lane + 128)
            s = scores[:, lanes] * SCALE + bias[i, :, lanes]
            e = jnp.exp(s - jnp.max(s, axis=0, keepdims=True))
            a = e * (1.0 / jnp.sum(e, axis=0, keepdims=True))
            attn[w, :, lanes] = a
            attn_low[w, :, lanes] = a.astype(BF16)
        value_t = value.astype(F32).T.astype(BF16)
        per_head = dot(value_t, attn_low[w]).astype(BF16) * heads_t[...]
        mixed[rows, :] = dot(rep_t[...], per_head, NT).astype(BF16)
    big2[:, 0:C] = dot(mixed[...], wo[...])
    for start in range(0, TOK, step):
        rows = slice(start, start + step)
        residual = (xs[rows, :] + big2[rows, 0:C]).astype(BF16).astype(F32)
        scaled, inverse = norm(residual)
        scaled_mid[rows, :] = scaled
        inv_mid[rows, :] = inverse
        normed_mid[rows, :] = (scaled * g2[...]).astype(BF16)
    edges[1].finish()
    for i in range(2):
        cs[i * HALF : (i + 1) * HALF, :] = dot(order[...], gathered_pieces(c_got, i)).astype(BF16)
    big[...] = dot(normed_mid[...], we[...])
    big2[...] = dot(cs[...], ws[...])
    for start in range(0, TOK, 16):
        rows = slice(start, start + 16)
        activated, slope = activation(big[rows, :])
        act[rows, :] = activated.astype(BF16)
        gexp[rows, :] = (big2[rows, :] * slope).astype(BF16)
    d_wide[:, 0:HID] = dot(normed_mid[...], gexp[...], TN)
    d_wide[:, HID : 2 * HID] = dot(cs[...], act[...], TN)
    for t in range(12):
        m_sum.pay[t * C : (t + 1) * C, :] = d_wide[:, t * 128 : (t + 1) * 128].astype(BF16)
    m_sum.core_start()
    big[:, 0:C] = dot(gexp[...], we[...], NT)
    gain_sum = jnp.zeros((1, C), F32)
    for start in range(0, TOK, step):
        rows = slice(start, start + step)
        grad = big[rows, 0:C]
        scaled = scaled_mid[rows, :]
        gain_sum = gain_sum + jnp.sum(grad * scaled, axis=0, keepdims=True)
        gres[rows, :] = norm_back(grad * g2[...], scaled, inv_mid[rows, :]) + cs[rows, :].astype(F32)
    gains[1:2, 0:C] = gain_sum
    grad_low = gres[...].astype(BF16)
    d_wide[:, 3 * C : 4 * C] = dot(mixed[...], grad_low, TN)
    gmix[...] = dot(grad_low, wo[...], NT).astype(BF16)
    m_sum.core_finish()
    m_sum.scatter_start()
    for w in range(4):
        rows = slice(w * WIN, (w + 1) * WIN)
        i = w // 2
        key, value = packed[1, rows, :], packed[2, rows, :]
        m_stack[...] = dot(rep[...], gmix[rows, :]).astype(BF16) * heads[...]
        gpack[2, rows, :] = dot(attn_low[w], m_stack[...]).astype(BF16)
        scores[...] = dot(value, m_stack[...], NT)
        for lane in range(0, LANESP, 128):
            lanes = slice(lane, lane + 128)
            a = attn[w, :, lanes]
            da = scores[:, lanes]
            ds = a * (da - jnp.sum(da * a, axis=0, keepdims=True))
            scores_low[:, lanes] = (ds * SCALE).astype(BF16)
            if w % 2 == 0:
                grad_scores[:, lanes] = ds
            else:
                grad_scores[:, lanes] = grad_scores[:, lanes] + ds
        gpack[1, rows, :] = dot(scores_low[...], q_stack[w]).astype(BF16)
        key_t = key.astype(F32).T.astype(BF16)
        per_head = dot(key_t, scores_low[...]).astype(BF16) * heads_t[...]
        gpack[0, rows, :] = dot(rep_t[...], per_head, NT).astype(BF16)
        if w % 2 == 1:
            gacc[...] = jnp.zeros_like(gacc)
            for b in range(WLON):
                start = (WLON - 1 - b) * 72
                gacc[0:ZA, start : start + LANES] = (
                    gacc[0:ZA, start : start + LANES] + grad_scores[b * ZA : (b + 1) * ZA, 0:LANES]
                )
            own_head = wide_codes[0:1, :]
            for h in range(HEADS):
                place = (i * HEADS + h) * ZA
                wt[place : place + ZA, :] = jnp.where(own_head == h, gacc[0:ZA, :], 0.0)
    m_sum.scatter_finish()
    m_sum.exchange_start()
    folded = dot(wt[...].astype(BF16), spread_t[...]).astype(BF16)
    tmask[...] = dot(folded, onehot[...])
    mine = lax.broadcasted_iota(jnp.int32, (ZA, POSP), 0) == pos_codes[1:2, :]
    for k in range(2 * HEADS):
        tsel[k : k + 1, :] = jnp.sum(
            jnp.where(mine, tmask[k * ZA : (k + 1) * ZA, :], 0.0), axis=0, keepdims=True
        )
    lane = lax.broadcasted_iota(jnp.int32, (1, POSP), 1)
    for i in range(2):
        mark = jnp.where(lane - POS == kinds[i, 0], 1.0, 0.0)
        rows = slice(i * HEADS, (i + 1) * HEADS)
        tsel[rows, :] = jnp.where(lane >= POS, mark, tsel[rows, :])
    gconv[...] = jnp.zeros_like(gconv)
    for t in range(26):
        gconv[t * ZA : (t + 1) * ZA, :] = tsel[0:ZA, t * 128 : (t + 1) * 128]
    b_sum.pay[...] = gconv[...].astype(BF16)
    b_sum.core_start()
    back = None
    for part in range(3):
        lanes = slice(part * C, (part + 1) * C)
        d_wide[:, lanes] = dot(normed_in[...], gpack[part], TN)
        term = dot(gpack[part], wa[:, lanes], NT)
        back = term if back is None else back + term
    big[:, 0:C] = back
    for t in range(6):
        t_sum.pay[t * C : (t + 1) * C, :] = d_wide[:, t * 128 : (t + 1) * 128].astype(BF16)
    t_sum.pay[6 * C : 1280, :] = jnp.zeros((128, 128), BF16)
    gain_sum = jnp.zeros((1, C), F32)
    for start in range(0, TOK, step):
        rows = slice(start, start + step)
        grad = big[rows, 0:C]
        scaled = scaled_in[rows, :]
        gain_sum = gain_sum + jnp.sum(grad * scaled, axis=0, keepdims=True)
        result = norm_back(grad * g1[...], scaled, inv_in[rows, :]) + gres[rows, :]
        act[rows, 0:C] = result.astype(BF16)
    gains[0:1, 0:C] = gain_sum
    t_sum.pay[6 * C : 6 * C + 16, :] = gains[:, 0:128].astype(BF16)
    t_sum.pay[6 * C + 16 : 6 * C + 32, 0:64] = gains[:, 128:192].astype(BF16)
    t_sum.core_start()
    for i in range(2):
        pieces = dot(order_t[...], act[i * HALF : (i + 1) * HALF, 0:C]).astype(BF16)
        spread_pieces(push_out, pieces, i)
    edge_out[0:224, :] = push_out[0:224, :]
    push = Edges(me, push_out, edge_out, sems, 6, 1)
    push.start()
    b_sum.core_finish()
    b_sum.scatter_start()
    t_sum.core_finish()
    t_sum.scatter_start()
    m_sum.exchange_finish()
    m_sum.gather_start()
    b_sum.scatter_finish()
    b_sum.exchange_start()
    t_sum.scatter_finish()
    t_sum.exchange_start()
    m_sum.gather_finish()
    m_sum.back_start()
    b_sum.exchange_finish()
    b_sum.gather_start()
    t_sum.exchange_finish()
    t_sum.gather_start()
    m_sum.back_finish()
    push.finish()
    outs = [
        pltpu.make_async_copy(edge_out, edge_hbm, local.at[0]),
        pltpu.make_async_copy(m_sum.full, m_hbm, local.at[1]),
    ]
    for copy in outs:
        copy.start()
    b_sum.gather_finish()
    b_sum.back_start()
    t_sum.gather_finish()
    t_sum.back_start()
    b_sum.back_finish()
    last = pltpu.make_async_copy(b_sum.full, b_hbm, local.at[2])
    last.start()
    outs.append(last)
    t_sum.back_finish()
    last = pltpu.make_async_copy(t_sum.full, t_hbm, local.at[3])
    last.start()
    outs.append(last)
    for copy in outs:
        copy.wait()


def summed_scratch(n):
    return [
        pltpu.VMEM((16 * n, 128), BF16),
        pltpu.VMEM((8 * n, 128), BF16),
        pltpu.VMEM((7, n, 128), BF16),
        pltpu.VMEM((8, n, 128), BF16),
        pltpu.VMEM((16 * n, 128), BF16),
    ]


def local_scratch():
    return [
        pltpu.VMEM((16, POSP), F32),
        pltpu.VMEM((WIN, POSP), F32),
        pltpu.VMEM((WIN, WIDEP), F32),
        pltpu.VMEM((2, 16, WIDEP), F32),
        pltpu.VMEM((CODESP, POSP), BF16),
        pltpu.VMEM((2, WIN, LANESP), F32),
        pltpu.VMEM((TOK, C), F32),
        pltpu.VMEM((TOK, C), BF16),
        pltpu.VMEM((TOK, C), F32),
        pltpu.VMEM((TOK, 1), F32),
        pltpu.VMEM((TOK, C), BF16),
        pltpu.VMEM((3, TOK, C), BF16),
        pltpu.VMEM((4, LANESP, C), BF16),
        pltpu.VMEM((WIN, LANESP), F32),
        pltpu.VMEM((4, WIN, LANESP), F32),
        pltpu.VMEM((4, WIN, LANESP), BF16),
        pltpu.VMEM((TOK, C), BF16),
        pltpu.VMEM((TOK, C), F32),
        pltpu.VMEM((TOK, 1), F32),
        pltpu.VMEM((TOK, C), BF16),
        pltpu.VMEM((TOK, HID), F32),
        pltpu.VMEM((TOK, HID), F32),
        pltpu.VMEM((TOK, HID), BF16),
        pltpu.VMEM((TOK, HID), BF16),
        pltpu.VMEM((TOK, C), F32),
        pltpu.VMEM((TOK, C), BF16),
        pltpu.VMEM((LANESP, C), BF16),
        pltpu.VMEM((WIN, LANESP), F32),
        pltpu.VMEM((WIN, LANESP), BF16),
        pltpu.VMEM((3, TOK, C), BF16),
        pltpu.VMEM((16, WIDEP), F32),
        pltpu.VMEM((384, 128), F32),
        pltpu.VMEM((16, 256), F32),
        pltpu.VMEM((C, 2 * HID), F32),
        *[pltpu.VMEM((640, C), BF16)] * 6,
        *summed_scratch(144),
        *summed_scratch(80),
        pltpu.VMEM((384, 128), BF16),
        pltpu.VMEM((384, 128), BF16),
        pltpu.VMEM((7, 48, 128), BF16),
        pltpu.VMEM((48, 128), BF16),
        pltpu.VMEM((3072, 128), BF16),
        pltpu.SemaphoreType.DMA((2, 80)),
        pltpu.SemaphoreType.DMA((4,)),
    ]


def final_constants():
    col = np.arange(384)
    col_o, col_h = col % 48 // 12, col % 6
    row_o, row_h, row_t = col // 96, col // 16 % 6, col % 16
    same = (row_o[:, None] == col_o[None, :]) & (row_h[:, None] == col_h[None, :])
    pick = np.arange(128)[None, :] == (112 + row_t)[:, None]
    share = (col // 48 * 48 + 12 + col % 12)[:, None] == col[None, :]
    low = lambda a: jnp.asarray(a.astype(np.float32), BF16)
    return low(same), low(pick / 16.0), low(share)


def finish(edge, m, t, b, grid_t, same, pick, share, gx, gains, d_attend, d_output, d_expand, d_shrink, table):
    factor = 1.0 / math.sqrt(TOK * 128)
    for j in range(6):
        d_expand[:, j * 128 : (j + 1) * 128] = m[j * C : (j + 1) * C, :].astype(F32) * factor
        d_shrink[:, j * 128 : (j + 1) * 128] = m[(j + 6) * C : (j + 7) * C, :].astype(F32) * factor
    for j in range(4):
        d_attend[:, j * 128 : (j + 1) * 128] = t[j * C : (j + 1) * C, :].astype(F32) * factor
    d_attend[:, 512:576] = t[4 * C : 5 * C, 0:64].astype(F32) * factor
    d_output[:, 0:64] = t[4 * C : 5 * C, 64:128].astype(F32) * factor
    d_output[:, 64:192] = t[5 * C : 6 * C, :].astype(F32) * factor
    gains[:, 0:128] = t[6 * C : 6 * C + 16, :].astype(F32) * factor
    gains[:, 128:256] = t[6 * C + 16 : 6 * C + 32, :].astype(F32) * factor
    for i in range(2):
        result = dot(grid_t[...], gathered_pieces(edge, i)).astype(BF16)
        if i == 0:
            gx[144:432, :] = result
        else:
            gx[432:576, :] = result[0:144, :]
            gx[0:144, :] = result[144:288, :]

    def block_of(s):
        return jnp.concatenate([b[(c * 8 + s) * 192 : (c * 8 + s) * 192 + 192, :] for c in range(2)], axis=0)

    kinds = dot(share[...], block_of(6)).astype(BF16)
    choose = dot(pick[...], kinds, NT).astype(BF16) * same[...]
    for s in range(7):
        part = dot(choose, block_of(s))
        for o in range(4):
            lo = (4 * s + o) * 128
            if lo >= POSP:
                continue
            width = min(128, POS - lo)
            for h in range(HEADS):
                table[h, :, lo : lo + width] = part[o * 96 + h * 16 : o * 96 + h * 16 + 16, 0:width]


def body(
    fields, cotangent, window_kinds, first_gain, attend_weight, output_weight,
    second_gain, expand_weight, shrink_weight, bias_table,
):
    vm, hbm = pl.BlockSpec(memory_space=pltpu.VMEM), pl.BlockSpec(memory_space=pl.ANY)
    consts = constants()
    sent = pl.pallas_call(
        block,
        out_shape=[jax.ShapeDtypeStruct(s, BF16) for s in ((640, C), (2304, 128), (1280, 128), (3072, 128))],
        in_specs=[pl.BlockSpec(memory_space=pltpu.SMEM)] + [vm] * 20,
        out_specs=[hbm] * 4,
        scratch_shapes=local_scratch(),
        compiler_params=pltpu.CompilerParams(
            vmem_limit_bytes=60 * 2**20, collective_id=0, has_side_effects=True
        ),
        name="block_backward",
    )(
        window_kinds, fields.reshape(TOK, C), cotangent.reshape(TOK, C), first_gain[None], attend_weight,
        output_weight, second_gain[None], expand_weight, shrink_weight.T, bias_table.transpose(1, 0, 2), *consts,
    )
    shapes = [
        ((TOK, C), BF16), ((16, 256), F32), ((C, 3 * C), F32), ((C, C), F32),
        ((C, HID), F32), ((C, HID), F32), ((HEADS, TYPES, POS), F32),
    ]
    gx, gains, d_attend, d_output, d_expand, d_shrink, table = pl.pallas_call(
        finish,
        out_shape=[jax.ShapeDtypeStruct(s, d) for s, d in shapes],
        in_specs=[vm] * 8,
        out_specs=[vm] * 7,
        compiler_params=pltpu.CompilerParams(vmem_limit_bytes=40 * 2**20),
        name="finish",
    )(*sent, consts[-1].T, *final_constants())
    return (
        gx.reshape(LEV, ROWS, COLS, C), gains[0, :C], d_attend, d_output, gains[1, :C],
        d_expand, d_shrink.T, table.transpose(1, 0, 2),
    )


def solution(mesh):
    cells = P(None, "lat", "lon", None)
    in_specs = (cells, cells, P(None, "lat")) + (P(),) * 7
    out_specs = (cells,) + (P(),) * 7
    return jax.shard_map(body, mesh=mesh, in_specs=in_specs, out_specs=out_specs, check_vma=False)
```

```python
import functools
import math

import jax
import jax.numpy as jnp
import numpy as np
from jax import lax
from jax.experimental import pallas as pl
from jax.experimental.pallas import tpu as pltpu
from jax.sharding import PartitionSpec as P

F32, BF16 = jnp.float32, jnp.bfloat16
C, HEADS, HID = 192, 6, 768
WZ, WLAT, WLON = 2, 6, 12
LEV, ROWS, COLS = 4, 6, 24
POS, POSP = 3312, 3328
TYPES = 16
WIN = WZ * WLAT * WLON
ZA = WZ * WLAT
DIFFS = 2 * WLON - 1
LANES, LANESP = HEADS * WIN, 896
WIDE, WIDEP = DIFFS * HEADS * ZA, 1664
CODES, CODESP = DIFFS * ZA, 288
TOK = LEV * ROWS * COLS
HALF = TOK // 2
SCALE = (C // HEADS) ** (-0.5)
EPS = 1e-05


def constants():
    lane = np.arange(LANESP)
    lane_b, lane_h, lane_za = lane // 72, (lane // 12) % 6, lane % 12
    real = lane < LANES
    rep = ((lane_b * 12 + lane_za)[:, None] == np.arange(WIN)[None, :]) & real[:, None]
    heads = (lane_h[:, None] == (np.arange(C) // 32)[None, :]) & real[:, None]
    pos = np.arange(POSP)
    diff, rest = pos % DIFFS, pos // DIFFS
    aq, ap, zq, zp = rest % 6, rest // 6 % 6, rest // 36 % 2, rest // 72
    fine = pos < POS
    code = np.where(fine, diff * ZA + zp * 6 + ap, -1)
    rho = np.where(fine, zq * 6 + aq, -1)
    pos_codes = rho[None, :].astype(np.int32)
    picks = np.arange(CODESP)[:, None] == code[None, :]
    wide = np.arange(WIDEP)
    wide_r, wide_h, wide_za = wide // 72, (wide // 12) % 6, wide % 12
    okay = wide < WIDE
    spread = ((wide_r * 12 + wide_za)[None, :] == np.arange(CODESP)[:, None]) & okay[None, :]
    wide_codes = np.stack(
        [np.where(okay, wide_h, -1), wide_za // 6, (wide_za % 6) // 3]
    ).astype(np.int32)
    cell = np.arange(HALF)
    lon, z, a = cell // ZA, cell % ZA // 6, cell % 6
    place = np.where(
        a < 3,
        np.where(lon < 18, (z * 3 + a) * 18 + lon, 112 + (z * 3 + a) * 6 + lon - 18),
        np.where(lon < 18, 160 + (z * 3 + a - 3) * 18 + lon, 272 + (z * 3 + a - 3) * 6 + lon - 18),
    )
    order = place[:, None] == np.arange(320)[None, :]
    z, a, lon = cell // 144, cell % 144 // 24, cell % 24
    place = np.where(
        a >= 3,
        np.where(lon >= 6, (z * 3 + a - 3) * 18 + lon - 6, 112 + (z * 3 + a - 3) * 6 + lon),
        np.where(lon >= 6, 160 + (z * 3 + a) * 18 + lon - 6, 272 + (z * 3 + a) * 6 + lon),
    )
    grid = np.arange(320)[:, None] == place[None, :]
    low = lambda a: jnp.asarray(a.astype(np.float32), BF16)
    return (
        low(rep), low(rep.T), low(heads), low(heads.T),
        jnp.asarray(pos_codes), jnp.asarray(wide_codes), low(spread), low(spread.T), low(order), low(order.T), low(grid),
        low(picks), low(picks.T),
    )


def dot(a, b, dims=((1,), (0,))):
    return lax.dot_general(a, b, (dims, ((), ())), preferred_element_type=F32)


NT = ((1,), (1,))
TN = ((0,), (0,))


def split2(v):
    hi = v.astype(BF16)
    return hi, (v - hi.astype(F32)).astype(BF16)


def norm(values):
    center = values - jnp.mean(values, axis=-1, keepdims=True)
    inverse = lax.rsqrt(jnp.mean(center * center, axis=-1, keepdims=True) + EPS)
    return center * inverse, inverse


def norm_back(weighted, scaled, inverse):
    return inverse * (
        weighted
        - jnp.mean(weighted, axis=-1, keepdims=True)
        - scaled * jnp.mean(weighted * scaled, axis=-1, keepdims=True)
    )


def activation(values):
    normal_cdf = 0.5 * (1.0 + lax.erf(values * 0.7071067811865476))
    density = jnp.exp(-0.5 * values * values) * 0.3989422804014327
    return values * normal_cdf, normal_cdf + values * density


def prepare_bias(lat, kinds, table, pos_codes, wide_codes, spread, picks_t, tmask, wt, wall, bias):
    mine = lax.broadcasted_iota(jnp.int32, (16, POS), 0) == pos_codes[0:1, 0:POS]
    tmask[:, 3200:POSP] = jnp.zeros((2 * 192, 128), BF16)
    for i in range(2):
        for h in range(HEADS):
            values = table[h, pl.ds(kinds[0, i], 1), :]
            k = i * HEADS + h
            high = values.astype(BF16).astype(F32)
            for part, piece in enumerate((high, values - high)):
                start = part * 192 + k * 16
                tmask[start : start + 16, 0:POS] = jnp.where(mine, piece, 0.0).astype(BF16)
    both = dot(tmask[...], picks_t[...])
    coded = both[0:192, :] + both[192:384, :]
    both = dot(jnp.concatenate(split2(coded), axis=0), spread[...])
    wt[...] = both[0:192, :] + both[192:384, :]
    own_head = wide_codes[0:1, :]
    row_id = lax.broadcasted_iota(jnp.int32, (ZA, WIDEP), 0)
    row_z = (row_id >= 6).astype(jnp.int32)
    row_a = row_id - 6 * row_z
    level_cut = row_z != wide_codes[1:2, :]
    row_cut = (row_a >= 3).astype(jnp.int32) != wide_codes[2:3, :]
    last = jnp.full((ZA, WIDEP), lat, jnp.int32) == lax.axis_size("lat") - 1
    bias[...] = jnp.zeros_like(bias)
    for i in range(2):
        acc = jnp.zeros((ZA, WIDEP), F32)
        for h in range(HEADS):
            start = (i * HEADS + h) * 16
            acc = acc + jnp.where(own_head == h, wt[start : start + ZA, :], 0.0)
        cut = row_cut & last
        if i == 1:
            cut = cut | level_cut
        wall[i, 0:ZA, :] = jnp.where(cut, -1e30, acc)
        for b in range(WLON):
            start = (WLON - 1 - b) * 72
            bias[i, b * ZA : (b + 1) * ZA, 0:LANES] = wall[i, 0:ZA, start : start + LANES]


MESH = pl.DeviceIdType.MESH


class Place:
    def __init__(self):
        self.lon, self.lat = lax.axis_index("lon"), lax.axis_index("lat")
        self.core = lax.rem(self.lon, 2)
        self.ring = lax.div(self.lon, 2)

    def twin(self):
        return (self.lon + 1 - 2 * self.core, self.lat)

    def ring_at(self, k):
        return lax.rem(self.ring + k, 8)

    def ring_peer(self, k):
        return (self.ring_at(k) * 2 + self.core, self.lat)

    def fold_lat(self, k):
        near = lax.div(self.ring_at(k), 4) == lax.div(self.ring, 4)
        return jnp.where(near, self.lat, self.lat + 1 - 2 * lax.rem(self.lat, 2))

    def fold_peer(self, k):
        return (self.ring_at(k) * 2 + self.core, self.fold_lat(k))

    def lat_peer(self, k):
        return (self.lon, lax.rem(self.lat + k, 8))

    def beside(self, east, north):
        return (lax.rem(self.lon + 16 + east, 16), lax.rem(self.lat + 8 + north, 8))


def greet(me):
    others = [me.twin()]
    others += [me.ring_peer(k) for k in range(1, 8)] + [me.lat_peer(k) for k in range(1, 8)]
    others += [me.fold_peer(k) for k in range(1, 8)]
    others += [me.beside(1, 0), me.beside(-1, 0), me.beside(1, 1), me.beside(-1, -1)]
    barrier = pltpu.get_barrier_semaphore()
    for other in others:
        pl.semaphore_signal(barrier, inc=1, device_id=other, device_id_type=MESH)
    return lambda: pl.semaphore_wait(barrier, len(others))


def remote(src, dst, sems, index, device):
    return pltpu.make_async_remote_copy(
        src_ref=src, dst_ref=dst, send_sem=sems.at[0, index], recv_sem=sems.at[1, index],
        device_id=device, device_id_type=MESH,
    )


class Edges:
    def __init__(self, me, src, dst, sems, base, by):
        pieces = ((224, 320, (by, 0)), (320, 544, (0, by)), (544, 640, (by, by)))
        self.copies = [
            remote(src.at[pl.ds(lo, hi - lo)], dst.at[pl.ds(lo, hi - lo)], sems, base + j, me.beside(*way))
            for j, (lo, hi, way) in enumerate(pieces)
        ]

    def start(self):
        for copy in self.copies:
            copy.start()

    def finish(self):
        for copy in self.copies:
            copy.wait()


EDGE_PARTS = ((0, 112, 0), (112, 160, 224), (160, 272, 320), (272, 320, 544))


def spread_pieces(dst, pieces, i):
    for lo, hi, base in EDGE_PARTS:
        n = hi - lo
        dst[base + i * n : base + (i + 1) * n, :] = pieces[lo:hi, :]


def gathered_pieces(src, i):
    return jnp.concatenate(
        [src[base + i * (hi - lo) : base + (i + 1) * (hi - lo), :] for lo, hi, base in EDGE_PARTS], axis=0
    )


def flat_spans(start, n):
    done = 0
    while done < n:
        share, off = divmod(start + done, 80)
        size = min(80 - off, n - done)
        yield done, size, share, off
        done += size


def put_flat(pay, start, values):
    for done, size, share, off in flat_spans(start, values.shape[0]):
        pay[share * 112 + off : share * 112 + off + size, :] = values[done : done + size, :]


def span(ref, start, n):
    return ref.at[pl.ds(pl.multiple_of(start, 16), n)]


class Summed:
    def __init__(self, me, sems, base, n, pay, arrived, first, second, full):
        self.me, self.sems, self.base, self.n = me, sems, base, n
        self.pay, self.arrived, self.first, self.second, self.full = pay, arrived, first, second, full

    def core_start(self):
        n = self.n
        self.core_copy = remote(
            span(self.pay, (1 - self.me.core) * 8 * n, 8 * n), self.arrived, self.sems, self.base, self.me.twin()
        )
        self.core_copy.start()

    def core_finish(self):
        self.core_copy.wait()
        n = self.n
        for s in range(8):
            place = pl.ds(pl.multiple_of(self.me.core * 8 * n + s * n, 16), n)
            mine = self.pay[place, :].astype(F32) + self.arrived[s * n : (s + 1) * n, :].astype(F32)
            self.pay[place, :] = mine.astype(BF16)

    def first_peer(self, k):
        return self.me.fold_peer(k)

    def scatter_start(self):
        me, n = self.me, self.n
        self.scatter = [
            remote(
                span(self.pay, (me.core * 8 + me.ring_at(k)) * n, n), self.first.at[k - 1],
                self.sems, self.base + k, self.first_peer(k),
            )
            for k in range(1, 8)
        ]
        for copy in self.scatter:
            copy.start()

    def scattered(self):
        me, n = self.me, self.n
        total = self.pay[pl.ds(pl.multiple_of((me.core * 8 + me.ring) * n, 16), n), :].astype(F32)
        for copy in self.scatter:
            copy.wait_recv()
        for k in range(7):
            total = total + self.first[k].astype(F32)
        return total.astype(BF16)

    def scatter_finish(self):
        self.second[self.me.lat] = self.scattered()

    def exchange_start(self):
        me = self.me
        self.exchange = [
            remote(self.second.at[me.lat], self.second.at[me.lat], self.sems, self.base + 7 + k, me.lat_peer(k))
            for k in range(1, 8)
        ]
        for copy in self.exchange:
            copy.start()

    def exchanged(self, summed):
        for copy in self.exchange:
            copy.wait_recv()
        total = self.second[0, 0:summed, :].astype(F32)
        for k in range(1, 8):
            total = total + self.second[k, 0:summed, :].astype(F32)
        return total.astype(BF16)

    def exchange_finish(self):
        me, n = self.me, self.n
        self.full[pl.ds(pl.multiple_of((me.core * 8 + me.ring) * n, 16), n), :] = self.exchanged(n)

    def gather_start(self):
        me, n = self.me, self.n
        own = span(self.full, (me.core * 8 + me.ring) * n, n)
        self.gather = [
            remote(own, own, self.sems, self.base + 14 + k, me.fold_peer(k)) for k in range(1, 8)
        ]
        for copy in self.gather:
            copy.start()

    def gather_finish(self):
        for copy in self.gather:
            copy.wait_recv()

    def back_start(self):
        half = span(self.full, self.me.core * 8 * self.n, 8 * self.n)
        self.back = [remote(half, half, self.sems, self.base + 22, self.me.twin())]
        self.back[0].start()

    def back_finish(self):
        for copy in self.back:
            copy.wait()
        for copy in self.scatter + self.exchange + self.gather:
            copy.wait_send()


class Mixed(Summed):
    def __init__(self, me, sems, base, pay, arrived, first, second, full, other):
        super().__init__(me, sems, base, 112, pay, arrived, first, second, full)
        self.other = other

    def first_peer(self, k):
        return self.me.ring_peer(k)

    def other_at(self, lat):
        return ((self.me.core * 8 + lat) * 8 + self.me.ring) * 16

    def scatter_finish(self):
        total = self.scattered()
        self.second[self.me.lat] = total[0:96, :]
        self.other[pl.ds(pl.multiple_of(self.other_at(self.me.lat), 16), 16), :] = total[96:112, :]

    def exchange_start(self):
        me = self.me
        super().exchange_start()
        self.spread = [
            remote(
                span(self.other, self.other_at(me.lat), 16), span(self.other, self.other_at(me.fold_lat(k)), 16),
                self.sems, self.base + 22 + k, me.fold_peer(k),
            )
            for k in range(1, 8)
        ]
        for copy in self.spread:
            copy.start()

    def exchange_finish(self):
        me = self.me
        start = (me.core * 8 + me.ring) * 208
        self.full[pl.ds(pl.multiple_of(start, 16), 80), :] = self.exchanged(80)
        for k in range(8):
            self.full[pl.ds(pl.multiple_of(start + 80 + k * 16, 16), 16), :] = self.second[k, 80:96, :]

    def gather_start(self):
        me = self.me
        own = span(self.full, (me.core * 8 + me.ring) * 208, 208)
        self.gather = [
            remote(own, own, self.sems, self.base + 14 + k, me.fold_peer(k)) for k in range(1, 8)
        ]
        for copy in self.gather:
            copy.start()
        for copy in self.spread:
            copy.wait_recv()
        mine = span(self.other, (me.core * 8 + me.lat) * 128, 128)
        more = [remote(mine, mine, self.sems, self.base + 29 + k, me.lat_peer(k)) for k in range(1, 8)]
        for copy in more:
            copy.start()
        self.gather += more

    def back_start(self):
        core = self.me.core
        halves = (span(self.full, core * 8 * 208, 8 * 208), span(self.other, core * 1024, 1024))
        self.back = [
            remote(half, half, self.sems, self.base + (22, 37)[j], self.me.twin()) for j, half in enumerate(halves)
        ]
        for copy in self.back:
            copy.start()

    def back_finish(self):
        super().back_finish()
        for copy in self.spread:
            copy.wait_send()


NAMES = (
    "x_in", "c_in", "grid", "g1", "table", "picks_t", "spread", "wide_codes", "pos_codes", "wa", "rep", "heads",
    "order", "heads_t", "rep_t", "wo", "g2", "we", "ws", "spread_t", "picks", "order_t",
)


def block(
    kinds, *refs
):
    count = len(NAMES)
    sources, (edge_hbm, m_hbm, t_hbm, o_hbm) = refs[:count], refs[count : count + 4]
    held = refs[count + 4 : 2 * count + 4]
    (
        tsel, tmask, wt, wall, bias, wide_low, flat,
        xs, cs, scaled_in, inv_in, normed_in, packed, q_stack, scores, attn, attn_low, mixed,
        scaled_mid, inv_mid, normed_mid, big, big2, act, gexp, gres, gmix, m_stack, grad_scores, scores_low,
        gpack, gacc, gconv, gains, d_wide,
        x_out, c_out, push_out, x_got, c_got, edge_out,
        m_pay, m_arrived, m_first, m_second, m_full,
        t_pay, t_arrived, t_first, t_second, t_full, t_other,
        sems, local, loads,
    ) = refs[2 * count + 4 :]
    (
        x_in, c_in, grid, g1, table, picks_t, spread, wide_codes, pos_codes, wa, rep, heads,
        order, heads_t, rep_t, wo, g2, we, ws, spread_t, picks, order_t,
    ) = held
    incoming = [pltpu.make_async_copy(a, b, loads.at[n]) for n, (a, b) in enumerate(zip(sources, held))]
    for copy in incoming:
        copy.start()
    me = Place()
    wait_all = greet(me)
    m_sum = Summed(me, sems, 9, 144, m_pay, m_arrived, m_first, m_second, m_full)
    t_sum = Mixed(me, sems, 32, t_pay, t_arrived, t_first, t_second, t_full, t_other)
    gains[...] = jnp.zeros_like(gains)
    gacc[...] = jnp.zeros_like(gacc)
    edges = [Edges(me, x_out, x_got, sems, 0, -1), Edges(me, c_out, c_got, sems, 3, -1)]
    for copy in incoming[0:3]:
        copy.wait()
    for n, (src, out) in enumerate(((x_in, x_out), (c_in, c_out))):
        spread_pieces(out, dot(grid[...], src[144:432, :]).astype(BF16), 0)
        ends = jnp.concatenate([src[432:576, :], src[0:144, :]], axis=0)
        spread_pieces(out, dot(grid[...], ends).astype(BF16), 1)
        if n == 0:
            wait_all()
        edges[n].start()
    x_got[0:224, :] = x_out[0:224, :]
    c_got[0:224, :] = c_out[0:224, :]
    for copy in incoming[3:]:
        copy.wait()
    prepare_bias(me.lat, kinds, table, pos_codes, wide_codes, spread, picks_t, tmask, wt, wall, bias)
    edges[0].finish()
    for i in range(2):
        xs[i * HALF : (i + 1) * HALF, :] = dot(order[...], gathered_pieces(x_got, i))
    step = 96
    for start in range(0, TOK, step):
        rows = slice(start, start + step)
        scaled, inverse = norm(xs[rows, :])
        scaled_in[rows, :] = scaled
        inv_in[rows, :] = inverse
        normed_in[rows, :] = (scaled * g1[...]).astype(BF16)
    for part in range(3):
        weight = wa[:, part * C : (part + 1) * C]
        packed[part] = dot(normed_in[...], weight).astype(BF16)
    for w in range(4):
        rows = slice(w * WIN, (w + 1) * WIN)
        i = w // 2
        query, key, value = packed[0, rows, :], packed[1, rows, :], packed[2, rows, :]
        q_stack[w] = dot(rep[...], query).astype(BF16) * heads[...]
        scores[...] = dot(key, q_stack[w], NT)
        for lane in range(0, LANESP, 128):
            lanes = slice(lane, lane + 128)
            s = scores[:, lanes] * SCALE + bias[i, :, lanes]
            e = jnp.exp(s - jnp.max(s, axis=0, keepdims=True))
            a = e * (1.0 / jnp.sum(e, axis=0, keepdims=True))
            attn[w, :, lanes] = a
            attn_low[w, :, lanes] = a.astype(BF16)
        value_t = value.astype(F32).T.astype(BF16)
        per_head = dot(value_t, attn_low[w]).astype(BF16) * heads_t[...]
        mixed[rows, :] = dot(rep_t[...], per_head, NT).astype(BF16)
    big2[:, 0:C] = dot(mixed[...], wo[...])
    for start in range(0, TOK, step):
        rows = slice(start, start + step)
        residual = (xs[rows, :] + big2[rows, 0:C]).astype(BF16).astype(F32)
        scaled, inverse = norm(residual)
        scaled_mid[rows, :] = scaled
        inv_mid[rows, :] = inverse
        normed_mid[rows, :] = (scaled * g2[...]).astype(BF16)
    edges[1].finish()
    for i in range(2):
        cs[i * HALF : (i + 1) * HALF, :] = dot(order[...], gathered_pieces(c_got, i)).astype(BF16)
    big[...] = dot(normed_mid[...], we[...])
    big2[...] = dot(cs[...], ws[...])
    for start in range(0, TOK, 16):
        rows = slice(start, start + 16)
        activated, slope = activation(big[rows, :])
        act[rows, :] = activated.astype(BF16)
        gexp[rows, :] = (big2[rows, :] * slope).astype(BF16)
    d_wide[:, 0:HID] = dot(normed_mid[...], gexp[...], TN)
    d_wide[:, HID : 2 * HID] = dot(cs[...], act[...], TN)
    for t in range(12):
        m_sum.pay[t * C : (t + 1) * C, :] = d_wide[:, t * 128 : (t + 1) * 128].astype(BF16)
    m_sum.core_start()
    big[:, 0:C] = dot(gexp[...], we[...], NT)
    gain_sum = jnp.zeros((1, C), F32)
    for start in range(0, TOK, step):
        rows = slice(start, start + step)
        grad = big[rows, 0:C]
        scaled = scaled_mid[rows, :]
        gain_sum = gain_sum + jnp.sum(grad * scaled, axis=0, keepdims=True)
        gres[rows, :] = norm_back(grad * g2[...], scaled, inv_mid[rows, :]) + cs[rows, :].astype(F32)
    gains[1:2, 0:C] = gain_sum
    grad_low = gres[...].astype(BF16)
    d_wide[:, 3 * C : 4 * C] = dot(mixed[...], grad_low, TN)
    gmix[...] = dot(grad_low, wo[...], NT).astype(BF16)
    m_sum.core_finish()
    m_sum.scatter_start()
    for w in range(4):
        rows = slice(w * WIN, (w + 1) * WIN)
        i = w // 2
        key, value = packed[1, rows, :], packed[2, rows, :]
        m_stack[...] = dot(rep[...], gmix[rows, :]).astype(BF16) * heads[...]
        gpack[2, rows, :] = dot(attn_low[w], m_stack[...]).astype(BF16)
        scores[...] = dot(value, m_stack[...], NT)
        for lane in range(0, LANESP, 128):
            lanes = slice(lane, lane + 128)
            a = attn[w, :, lanes]
            da = scores[:, lanes]
            ds = a * (da - jnp.sum(da * a, axis=0, keepdims=True))
            scores_low[:, lanes] = (ds * SCALE).astype(BF16)
            if w % 2 == 0:
                grad_scores[:, lanes] = ds
            else:
                grad_scores[:, lanes] = grad_scores[:, lanes] + ds
        gpack[1, rows, :] = dot(scores_low[...], q_stack[w]).astype(BF16)
        key_t = key.astype(F32).T.astype(BF16)
        per_head = dot(key_t, scores_low[...]).astype(BF16) * heads_t[...]
        gpack[0, rows, :] = dot(rep_t[...], per_head, NT).astype(BF16)
        if w % 2 == 1:
            gacc[...] = jnp.zeros_like(gacc)
            for b in range(WLON):
                start = (WLON - 1 - b) * 72
                gacc[0:ZA, start : start + LANES] = (
                    gacc[0:ZA, start : start + LANES] + grad_scores[b * ZA : (b + 1) * ZA, 0:LANES]
                )
            own_head = wide_codes[0:1, :]
            for h in range(HEADS):
                place = (i * HEADS + h) * 16
                wide_low[place : place + 16, :] = jnp.where(own_head == h, gacc[...], 0.0).astype(BF16)
    folded = dot(wide_low[...], spread_t[...]).astype(BF16)
    mine = lax.broadcasted_iota(jnp.int32, (16, POSP), 0) == pos_codes[0:1, :]
    flat[...] = dot(folded, picks[...])
    for k in range(2 * HEADS):
        tsel[k : k + 1, :] = jnp.sum(
            jnp.where(mine, flat[k * 16 : (k + 1) * 16, :], 0.0), axis=0, keepdims=True
        )
    lane = lax.broadcasted_iota(jnp.int32, (1, 128), 1)
    gconv[...] = jnp.zeros_like(gconv)
    for t in range(32):
        if t < 26:
            gconv[t * 16 : t * 16 + ZA, :] = tsel[0:ZA, t * 128 : (t + 1) * 128]
        for i in range(2):
            row = t * 16 + ZA + i
            gconv[row : row + 1, :] = jnp.where(lane == kinds[0, i], 1.0, 0.0)
    for k in range(16):
        t_sum.pay[k * 112 + 80 : k * 112 + 112, :] = gconv[k * 32 : k * 32 + 32, :].astype(BF16)
    back = None
    for part in range(3):
        lanes = slice(part * C, (part + 1) * C)
        d_wide[:, lanes] = dot(normed_in[...], gpack[part], TN)
        term = dot(gpack[part], wa[:, lanes], NT)
        back = term if back is None else back + term
    big[:, 0:C] = back
    for t in range(6):
        put_flat(t_sum.pay, t * C, d_wide[:, t * 128 : (t + 1) * 128].astype(BF16))
    put_flat(t_sum.pay, 6 * C, jnp.zeros((128, 128), BF16))
    gain_sum = jnp.zeros((1, C), F32)
    for start in range(0, TOK, step):
        rows = slice(start, start + step)
        grad = big[rows, 0:C]
        scaled = scaled_in[rows, :]
        gain_sum = gain_sum + jnp.sum(grad * scaled, axis=0, keepdims=True)
        result = norm_back(grad * g1[...], scaled, inv_in[rows, :]) + gres[rows, :]
        act[rows, 0:C] = result.astype(BF16)
    gains[0:1, 0:C] = gain_sum
    put_flat(t_sum.pay, 6 * C, gains[:, 0:128].astype(BF16))
    put_flat(t_sum.pay, 6 * C + 16, gains[:, 128:256].astype(BF16))
    m_sum.scatter_finish()
    m_sum.exchange_start()
    t_sum.core_start()
    for i in range(2):
        pieces = dot(order_t[...], act[i * HALF : (i + 1) * HALF, 0:C]).astype(BF16)
        spread_pieces(push_out, pieces, i)
    edge_out[0:224, :] = push_out[0:224, :]
    push = Edges(me, push_out, edge_out, sems, 6, 1)
    push.start()
    t_sum.core_finish()
    t_sum.scatter_start()
    m_sum.exchange_finish()
    m_sum.gather_start()
    t_sum.scatter_finish()
    t_sum.exchange_start()
    push.finish()
    outs = [pltpu.make_async_copy(edge_out, edge_hbm, local.at[0])]
    outs[0].start()
    t_sum.exchange_finish()
    t_sum.gather_start()
    m_sum.gather_finish()
    m_sum.back_start()
    m_sum.back_finish()
    outs.append(pltpu.make_async_copy(m_sum.full, m_hbm, local.at[1]))
    outs[1].start()
    t_sum.gather_finish()
    t_sum.back_start()
    t_sum.back_finish()
    outs.append(pltpu.make_async_copy(t_sum.full, t_hbm, local.at[2]))
    outs.append(pltpu.make_async_copy(t_sum.other, o_hbm, local.at[3]))
    for copy in outs[2:]:
        copy.start()
    for copy in outs:
        copy.wait()


def summed_scratch(n, second, full):
    return [
        pltpu.VMEM((16 * n, 128), BF16),
        pltpu.VMEM((8 * n, 128), BF16),
        pltpu.VMEM((7, n, 128), BF16),
        pltpu.VMEM((8, second, 128), BF16),
        pltpu.VMEM((16 * full, 128), BF16),
    ]


def local_scratch():
    return [
        pltpu.VMEM((16, POSP), F32),
        pltpu.VMEM((384, POSP), BF16),
        pltpu.VMEM((192, WIDEP), F32),
        pltpu.VMEM((2, 16, WIDEP), F32),
        pltpu.VMEM((2, WIN, LANESP), F32),
        pltpu.VMEM((192, WIDEP), BF16),
        pltpu.VMEM((192, POSP), F32),
        pltpu.VMEM((TOK, C), F32),
        pltpu.VMEM((TOK, C), BF16),
        pltpu.VMEM((TOK, C), F32),
        pltpu.VMEM((TOK, 1), F32),
        pltpu.VMEM((TOK, C), BF16),
        pltpu.VMEM((3, TOK, C), BF16),
        pltpu.VMEM((4, LANESP, C), BF16),
        pltpu.VMEM((WIN, LANESP), F32),
        pltpu.VMEM((4, WIN, LANESP), F32),
        pltpu.VMEM((4, WIN, LANESP), BF16),
        pltpu.VMEM((TOK, C), BF16),
        pltpu.VMEM((TOK, C), F32),
        pltpu.VMEM((TOK, 1), F32),
        pltpu.VMEM((TOK, C), BF16),
        pltpu.VMEM((TOK, HID), F32),
        pltpu.VMEM((TOK, HID), F32),
        pltpu.VMEM((TOK, HID), BF16),
        pltpu.VMEM((TOK, HID), BF16),
        pltpu.VMEM((TOK, C), F32),
        pltpu.VMEM((TOK, C), BF16),
        pltpu.VMEM((LANESP, C), BF16),
        pltpu.VMEM((WIN, LANESP), F32),
        pltpu.VMEM((WIN, LANESP), BF16),
        pltpu.VMEM((3, TOK, C), BF16),
        pltpu.VMEM((16, WIDEP), F32),
        pltpu.VMEM((512, 128), F32),
        pltpu.VMEM((16, 256), F32),
        pltpu.VMEM((C, 2 * HID), F32),
        *[pltpu.VMEM((640, C), BF16)] * 6,
        *summed_scratch(144, 144, 144),
        *summed_scratch(112, 96, 208),
        pltpu.VMEM((2048, 128), BF16),
        pltpu.SemaphoreType.DMA((2, 72)),
        pltpu.SemaphoreType.DMA((4,)),
        pltpu.SemaphoreType.DMA((len(NAMES),)),
    ]


def final_constants():
    col, row = np.arange(128), np.arange(96)
    same = (row[:, None] // 16 == col[None, :] % 16 % 6) & (col[None, :] % 16 < ZA)
    pick = col[None, :] == (row % 16)[:, None]
    source = np.where(col % 16 < ZA, col // 16 * 16 + ZA + col % 16 // 6, -1)
    share = source[:, None] == col[None, :]
    low = lambda a: jnp.asarray(a.astype(np.float32), BF16)
    return low(same), low(pick / 16.0), low(share)


def finish(
    edge_hbm, m_hbm, t_hbm, o_hbm, grid_hbm, same_hbm, pick_hbm, share_hbm,
    gx_hbm, first_hbm, second_hbm, attend_hbm, output_hbm, expand_hbm, shrink_hbm, table_hbm,
    edge, m, t, other, grid_t, same, pick, share,
    gx, d_first, d_second, d_attend, d_output, d_expand, d_shrink, table, loads, stores,
):
    factor = 1.0 / math.sqrt(TOK * 128)
    pairs = (
        (m_hbm, m), (t_hbm, t), (o_hbm, other), (share_hbm, share), (pick_hbm, pick), (same_hbm, same), (grid_hbm, grid_t),
        (edge_hbm, edge),
    )
    incoming = [pltpu.make_async_copy(src, dst, loads.at[j]) for j, (src, dst) in enumerate(pairs)]
    for copy in incoming:
        copy.start()
    outgoing = []

    def store(src, dst):
        copy = pltpu.make_async_copy(src, dst, stores.at[len(outgoing)])
        copy.start()
        outgoing.append(copy)

    incoming[0].wait()
    for j in range(6):
        d_expand[:, j * 128 : (j + 1) * 128] = m[j * C : (j + 1) * C, :].astype(F32) * factor
    store(d_expand, expand_hbm)
    for j in range(6):
        d_shrink[:, j * 128 : (j + 1) * 128] = m[(j + 6) * C : (j + 7) * C, :].astype(F32) * factor
    store(d_shrink, shrink_hbm)
    for copy in incoming[1:6]:
        copy.wait()

    def near_block(k):
        return t[k * 208 + 80 : k * 208 + 208, :]

    def far_block(k):
        starts = [((k // 8 * 8 + j) * 8 + k % 8) * 16 for j in range(8)]
        return jnp.concatenate([other[at : at + 16, :] for at in starts], axis=0)

    def choice(values):
        kinds = dot(share[...], values).astype(BF16)
        return dot(pick[...], kinds, NT).astype(BF16) * same[...]

    near, far = choice(near_block(0)), (choice(far_block(0)), choice(far_block(4)))
    for k in range(13):
        for o in range(2):
            part = dot(near, near_block(k)) if o == 0 else dot(far[k % 8 // 4], far_block(k))
            lo = (2 * k + o) * 128
            width = min(128, POS - lo)
            for h in range(HEADS):
                table[h, :, lo : lo + width] = part[h * 16 : h * 16 + 16, 0:width]
    store(table, table_hbm)

    def flat(start, n):
        return [
            (done, size, t[share_id * 208 + off : share_id * 208 + off + size, :].astype(F32) * factor)
            for done, size, share_id, off in flat_spans(start, n)
        ]

    for j in range(4):
        for done, size, values in flat(j * C, C):
            d_attend[done : done + size, j * 128 : (j + 1) * 128] = values
    for done, size, values in flat(4 * C, C):
        d_attend[done : done + size, 512:576] = values[:, 0:64]
        d_output[done : done + size, 0:64] = values[:, 64:128]
    store(d_attend, attend_hbm)
    for done, size, values in flat(5 * C, C):
        d_output[done : done + size, 64:192] = values
    store(d_output, output_hbm)
    low, high = flat(6 * C, 16)[0][2], flat(6 * C + 16, 16)[0][2]
    for row, dst, hbm in ((0, d_first, first_hbm), (1, d_second, second_hbm)):
        dst[:, 0:128] = low[row : row + 1, :]
        dst[:, 128:192] = high[row : row + 1, 0:64]
        store(dst, hbm)
    for copy in incoming[6:]:
        copy.wait()
    for i in range(2):
        result = dot(grid_t[...], gathered_pieces(edge, i)).astype(BF16)
        if i == 0:
            gx[144:432, :] = result
        else:
            gx[432:576, :] = result[0:144, :]
            gx[0:144, :] = result[144:288, :]
    store(gx, gx_hbm)
    for copy in outgoing:
        copy.wait()


def body(
    fields, cotangent, window_kinds, first_gain, attend_weight, output_weight,
    second_gain, expand_weight, shrink_weight, bias_table,
):
    hbm = pl.BlockSpec(memory_space=pl.ANY)
    consts = constants()
    named = dict(
        zip(
            ("rep", "rep_t", "heads", "heads_t", "pos_codes", "wide_codes", "spread", "spread_t", "order", "order_t",
             "grid", "picks", "picks_t"),
            consts,
        ),
        x_in=fields.reshape(TOK, C), c_in=cotangent.reshape(TOK, C), g1=first_gain[None], wa=attend_weight,
        wo=output_weight, g2=second_gain[None], we=expand_weight, ws=shrink_weight.T,
        table=bias_table.transpose(1, 0, 2),
    )
    operands = [named[name] for name in NAMES]
    sent = pl.pallas_call(
        block,
        out_shape=[jax.ShapeDtypeStruct(s, BF16) for s in ((640, C), (2304, 128), (3328, 128), (2048, 128))],
        in_specs=[pl.BlockSpec(memory_space=pltpu.SMEM)] + [hbm] * len(NAMES),
        out_specs=[hbm] * 4,
        scratch_shapes=[pltpu.VMEM(a.shape, a.dtype) for a in operands] + local_scratch(),
        compiler_params=pltpu.CompilerParams(
            vmem_limit_bytes=60 * 2**20, collective_id=0, has_side_effects=True
        ),
        name="block_backward",
    )(window_kinds.T, *operands)
    shapes = [
        ((TOK, C), BF16), ((1, C), F32), ((1, C), F32), ((C, 3 * C), F32), ((C, C), F32),
        ((C, HID), F32), ((C, HID), F32), ((HEADS, TYPES, POS), F32),
    ]
    inputs = [*sent, named["grid"].T, *final_constants()]
    gx, d_first, d_second, d_attend, d_output, d_expand, d_shrink, table = pl.pallas_call(
        finish,
        out_shape=[jax.ShapeDtypeStruct(s, d) for s, d in shapes],
        in_specs=[hbm] * 8,
        out_specs=[hbm] * 8,
        scratch_shapes=[
            *[pltpu.VMEM(a.shape, BF16) for a in inputs], *[pltpu.VMEM(s, d) for s, d in shapes],
            pltpu.SemaphoreType.DMA((8,)), pltpu.SemaphoreType.DMA((8,)),
        ],
        compiler_params=pltpu.CompilerParams(vmem_limit_bytes=60 * 2**20),
        name="finish",
    )(*inputs)
    return (
        gx.reshape(LEV, ROWS, COLS, C), d_first[0], d_attend, d_output, d_second[0],
        d_expand, d_shrink.T, table.transpose(1, 0, 2),
    )


def solution(mesh):
    cells = P(None, "lat", "lon", None)
    in_specs = (cells, cells, P(None, "lat")) + (P(),) * 7
    out_specs = (cells,) + (P(),) * 7
    return jax.shard_map(body, mesh=mesh, in_specs=in_specs, out_specs=out_specs, check_vma=False)
```

```python
import functools
import math

import jax
import jax.numpy as jnp
import numpy as np
from jax import lax
from jax.experimental import pallas as pl
from jax.experimental.pallas import tpu as pltpu
from jax.sharding import PartitionSpec as P

F32, BF16 = jnp.float32, jnp.bfloat16
C, HEADS, HID = 192, 6, 768
WZ, WLAT, WLON = 2, 6, 12
LEV, ROWS, COLS = 4, 6, 24
POS, POSP = 3312, 3328
TYPES = 16
WIN = WZ * WLAT * WLON
ZA = WZ * WLAT
DIFFS = 2 * WLON - 1
LANES, LANESP = HEADS * WIN, 896
WIDE, WIDEP = DIFFS * HEADS * ZA, 1664
CODES, CODESP = DIFFS * ZA, 288
TOK = LEV * ROWS * COLS
HALF = TOK // 2
SCALE = (C // HEADS) ** (-0.5)
EPS = 1e-05


def constants():
    lane = np.arange(LANESP)
    lane_b, lane_h, lane_za = lane // 72, (lane // 12) % 6, lane % 12
    real = lane < LANES
    rep = ((lane_b * 12 + lane_za)[:, None] == np.arange(WIN)[None, :]) & real[:, None]
    heads = (lane_h[:, None] == (np.arange(C) // 32)[None, :]) & real[:, None]
    pos = np.arange(POSP)
    diff, rest = pos % DIFFS, pos // DIFFS
    aq, ap, zq, zp = rest % 6, rest // 6 % 6, rest // 36 % 2, rest // 72
    fine = pos < POS
    code = np.where(fine, diff * ZA + zp * 6 + ap, -1)
    rho = np.where(fine, zq * 6 + aq, -1)
    pos_codes = rho[None, :].astype(np.int32)
    picks = np.arange(CODESP)[:, None] == code[None, :]
    wide = np.arange(WIDEP)
    wide_r, wide_h, wide_za = wide // 72, (wide // 12) % 6, wide % 12
    okay = wide < WIDE
    spread = ((wide_r * 12 + wide_za)[None, :] == np.arange(CODESP)[:, None]) & okay[None, :]
    wide_codes = np.stack(
        [np.where(okay, wide_h, -1), wide_za // 6, (wide_za % 6) // 3]
    ).astype(np.int32)
    cell = np.arange(HALF)
    lon, z, a = cell // ZA, cell % ZA // 6, cell % 6
    place = np.where(
        a < 3,
        np.where(lon < 18, (z * 3 + a) * 18 + lon, 112 + (z * 3 + a) * 6 + lon - 18),
        np.where(lon < 18, 160 + (z * 3 + a - 3) * 18 + lon, 272 + (z * 3 + a - 3) * 6 + lon - 18),
    )
    order = place[:, None] == np.arange(320)[None, :]
    z, a, lon = cell // 144, cell % 144 // 24, cell % 24
    place = np.where(
        a >= 3,
        np.where(lon >= 6, (z * 3 + a - 3) * 18 + lon - 6, 112 + (z * 3 + a - 3) * 6 + lon),
        np.where(lon >= 6, 160 + (z * 3 + a) * 18 + lon - 6, 272 + (z * 3 + a) * 6 + lon),
    )
    grid = np.arange(320)[:, None] == place[None, :]
    low = lambda a: jnp.asarray(a.astype(np.float32), BF16)
    return (
        low(rep), low(rep.T), low(heads), low(heads.T),
        jnp.asarray(pos_codes), jnp.asarray(wide_codes), low(spread), low(spread.T), low(order), low(order.T), low(grid),
        low(picks), low(picks.T),
    )


def dot(a, b, dims=((1,), (0,))):
    return lax.dot_general(a, b, (dims, ((), ())), preferred_element_type=F32)


NT = ((1,), (1,))
TN = ((0,), (0,))


def split2(v):
    hi = v.astype(BF16)
    return hi, (v - hi.astype(F32)).astype(BF16)


def norm(values):
    center = values - jnp.mean(values, axis=-1, keepdims=True)
    inverse = lax.rsqrt(jnp.mean(center * center, axis=-1, keepdims=True) + EPS)
    return center * inverse, inverse


def norm_back(weighted, scaled, inverse):
    return inverse * (
        weighted
        - jnp.mean(weighted, axis=-1, keepdims=True)
        - scaled * jnp.mean(weighted * scaled, axis=-1, keepdims=True)
    )


def activation(values):
    normal_cdf = 0.5 * (1.0 + lax.erf(values * 0.7071067811865476))
    density = jnp.exp(-0.5 * values * values) * 0.3989422804014327
    return values * normal_cdf, normal_cdf + values * density


def prepare_bias(lat, kinds, table, pos_codes, wide_codes, spread, picks_t, tmask, wt, wall, bias):
    mine = lax.broadcasted_iota(jnp.int32, (16, POS), 0) == pos_codes[0:1, 0:POS]
    tmask[:, 3200:POSP] = jnp.zeros((2 * 192, 128), BF16)
    for i in range(2):
        for h in range(HEADS):
            values = table[h, pl.ds(kinds[0, i], 1), :]
            k = i * HEADS + h
            high = values.astype(BF16).astype(F32)
            for part, piece in enumerate((high, values - high)):
                start = part * 192 + k * 16
                tmask[start : start + 16, 0:POS] = jnp.where(mine, piece, 0.0).astype(BF16)
    both = dot(tmask[...], picks_t[...])
    coded = both[0:192, :] + both[192:384, :]
    both = dot(jnp.concatenate(split2(coded), axis=0), spread[...])
    wt[...] = both[0:192, :] + both[192:384, :]
    own_head = wide_codes[0:1, :]
    row_id = lax.broadcasted_iota(jnp.int32, (ZA, WIDEP), 0)
    row_z = (row_id >= 6).astype(jnp.int32)
    row_a = row_id - 6 * row_z
    level_cut = row_z != wide_codes[1:2, :]
    row_cut = (row_a >= 3).astype(jnp.int32) != wide_codes[2:3, :]
    last = jnp.full((ZA, WIDEP), lat, jnp.int32) == lax.axis_size("lat") - 1
    bias[...] = jnp.zeros_like(bias)
    for i in range(2):
        acc = jnp.zeros((ZA, WIDEP), F32)
        for h in range(HEADS):
            start = (i * HEADS + h) * 16
            acc = acc + jnp.where(own_head == h, wt[start : start + ZA, :], 0.0)
        cut = row_cut & last
        if i == 1:
            cut = cut | level_cut
        wall[i, 0:ZA, :] = jnp.where(cut, -1e30, acc)
        for b in range(WLON):
            start = (WLON - 1 - b) * 72
            bias[i, b * ZA : (b + 1) * ZA, 0:LANES] = wall[i, 0:ZA, start : start + LANES]


MESH = pl.DeviceIdType.MESH


class Place:
    def __init__(self):
        self.lon, self.lat = lax.axis_index("lon"), lax.axis_index("lat")
        self.core = lax.rem(self.lon, 2)
        self.ring = lax.div(self.lon, 2)

    def twin(self):
        return (self.lon + 1 - 2 * self.core, self.lat)

    def ring_at(self, k):
        return lax.rem(self.ring + k, 8)

    def ring_peer(self, k):
        return (self.ring_at(k) * 2 + self.core, self.lat)

    def fold_lat(self, k):
        near = lax.div(self.ring_at(k), 4) == lax.div(self.ring, 4)
        return jnp.where(near, self.lat, self.lat + 1 - 2 * lax.rem(self.lat, 2))

    def fold_peer(self, k):
        return (self.ring_at(k) * 2 + self.core, self.fold_lat(k))

    def lat_peer(self, k):
        return (self.lon, lax.rem(self.lat + k, 8))

    def beside(self, east, north):
        return (lax.rem(self.lon + 16 + east, 16), lax.rem(self.lat + 8 + north, 8))


def greet(me):
    others = [me.twin()]
    others += [me.ring_peer(k) for k in range(1, 8)] + [me.lat_peer(k) for k in range(1, 8)]
    others += [me.fold_peer(k) for k in range(1, 8)]
    others += [me.beside(1, 0), me.beside(-1, 0), me.beside(1, 1), me.beside(-1, -1)]
    barrier = pltpu.get_barrier_semaphore()
    for other in others:
        pl.semaphore_signal(barrier, inc=1, device_id=other, device_id_type=MESH)
    return lambda: pl.semaphore_wait(barrier, len(others))


def remote(src, dst, sems, index, device):
    return pltpu.make_async_remote_copy(
        src_ref=src, dst_ref=dst, send_sem=sems.at[0, index], recv_sem=sems.at[1, index],
        device_id=device, device_id_type=MESH,
    )


class Edges:
    def __init__(self, me, src, dst, sems, base, by):
        pieces = ((224, 320, (by, 0)), (320, 544, (0, by)), (544, 640, (by, by)))
        self.copies = [
            remote(src.at[pl.ds(lo, hi - lo)], dst.at[pl.ds(lo, hi - lo)], sems, base + j, me.beside(*way))
            for j, (lo, hi, way) in enumerate(pieces)
        ]

    def start(self):
        for copy in self.copies:
            copy.start()

    def finish(self):
        for copy in self.copies:
            copy.wait()


EDGE_PARTS = ((0, 112, 0), (112, 160, 224), (160, 272, 320), (272, 320, 544))


def spread_pieces(dst, pieces, i):
    for lo, hi, base in EDGE_PARTS:
        n = hi - lo
        dst[base + i * n : base + (i + 1) * n, 0:C] = pieces[lo:hi, :]


def gathered_pieces(src, i):
    return jnp.concatenate(
        [src[base + i * (hi - lo) : base + (i + 1) * (hi - lo), 0:C] for lo, hi, base in EDGE_PARTS], axis=0
    )


def flat_spans(start, n):
    done = 0
    while done < n:
        share, off = divmod(start + done, 80)
        size = min(80 - off, n - done)
        yield done, size, share, off
        done += size


def put_flat(pay, start, values):
    for done, size, share, off in flat_spans(start, values.shape[0]):
        pay[share * 112 + off : share * 112 + off + size, :] = values[done : done + size, :]


def span(ref, start, n):
    return ref.at[pl.ds(pl.multiple_of(start, 16), n)]


class Summed:
    def __init__(self, me, sems, base, n, pay, arrived, first, second, full):
        self.me, self.sems, self.base, self.n = me, sems, base, n
        self.pay, self.arrived, self.first, self.second, self.full = pay, arrived, first, second, full

    def core_start(self):
        n = self.n
        self.core_copy = remote(
            span(self.pay, (1 - self.me.core) * 8 * n, 8 * n), self.arrived, self.sems, self.base, self.me.twin()
        )
        self.core_copy.start()

    def core_finish(self):
        self.core_copy.wait()
        n = self.n
        for s in range(8):
            place = pl.ds(pl.multiple_of(self.me.core * 8 * n + s * n, 16), n)
            mine = self.pay[place, :].astype(F32) + self.arrived[s * n : (s + 1) * n, :].astype(F32)
            self.pay[place, :] = mine.astype(BF16)

    def first_peer(self, k):
        return self.me.fold_peer(k)

    def scatter_start(self):
        me, n = self.me, self.n
        self.scatter = [
            remote(
                span(self.pay, (me.core * 8 + me.ring_at(k)) * n, n), self.first.at[k - 1],
                self.sems, self.base + k, self.first_peer(k),
            )
            for k in range(1, 8)
        ]
        for copy in self.scatter:
            copy.start()

    def scattered(self):
        me, n = self.me, self.n
        total = self.pay[pl.ds(pl.multiple_of((me.core * 8 + me.ring) * n, 16), n), :].astype(F32)
        for copy in self.scatter:
            copy.wait_recv()
        for k in range(7):
            total = total + self.first[k].astype(F32)
        return total.astype(BF16)

    def scatter_finish(self):
        self.second[self.me.lat] = self.scattered()

    def exchange_start(self):
        me = self.me
        self.exchange = [
            remote(self.second.at[me.lat], self.second.at[me.lat], self.sems, self.base + 7 + k, me.lat_peer(k))
            for k in range(1, 8)
        ]
        for copy in self.exchange:
            copy.start()

    def exchanged(self, summed):
        for copy in self.exchange:
            copy.wait_recv()
        total = self.second[0, 0:summed, :].astype(F32)
        for k in range(1, 8):
            total = total + self.second[k, 0:summed, :].astype(F32)
        return total.astype(BF16)

    def exchange_finish(self):
        me, n = self.me, self.n
        self.full[pl.ds(pl.multiple_of((me.core * 8 + me.ring) * n, 16), n), :] = self.exchanged(n)

    def gather_start(self):
        me, n = self.me, self.n
        own = span(self.full, (me.core * 8 + me.ring) * n, n)
        self.gather = [
            remote(own, own, self.sems, self.base + 14 + k, me.fold_peer(k)) for k in range(1, 8)
        ]
        for copy in self.gather:
            copy.start()

    def gather_finish(self):
        for copy in self.gather:
            copy.wait_recv()

    def back_start(self):
        half = span(self.full, self.me.core * 8 * self.n, 8 * self.n)
        self.back = [remote(half, half, self.sems, self.base + 22, self.me.twin())]
        self.back[0].start()

    def back_finish(self):
        for copy in self.back:
            copy.wait()
        for copy in self.scatter + self.exchange + self.gather:
            copy.wait_send()


class Mixed(Summed):
    def __init__(self, me, sems, base, pay, arrived, first, second, full, other):
        super().__init__(me, sems, base, 112, pay, arrived, first, second, full)
        self.other = other

    def first_peer(self, k):
        return self.me.ring_peer(k)

    def other_at(self, lat):
        return ((self.me.core * 8 + lat) * 8 + self.me.ring) * 16

    def scatter_finish(self):
        total = self.scattered()
        self.second[self.me.lat] = total[0:96, :]
        self.other[pl.ds(pl.multiple_of(self.other_at(self.me.lat), 16), 16), :] = total[96:112, :]

    def exchange_start(self):
        me = self.me
        super().exchange_start()
        self.spread = [
            remote(
                span(self.other, self.other_at(me.lat), 16), span(self.other, self.other_at(me.fold_lat(k)), 16),
                self.sems, self.base + 22 + k, me.fold_peer(k),
            )
            for k in range(1, 8)
        ]
        for copy in self.spread:
            copy.start()

    def exchange_finish(self):
        me = self.me
        start = (me.core * 8 + me.ring) * 208
        self.full[pl.ds(pl.multiple_of(start, 16), 80), :] = self.exchanged(80)
        for k in range(8):
            self.full[pl.ds(pl.multiple_of(start + 80 + k * 16, 16), 16), :] = self.second[k, 80:96, :]

    def gather_start(self):
        me = self.me
        own = span(self.full, (me.core * 8 + me.ring) * 208, 208)
        self.gather = [
            remote(own, own, self.sems, self.base + 14 + k, me.fold_peer(k)) for k in range(1, 8)
        ]
        for copy in self.gather:
            copy.start()
        for copy in self.spread:
            copy.wait_recv()
        mine = span(self.other, (me.core * 8 + me.lat) * 128, 128)
        more = [remote(mine, mine, self.sems, self.base + 29 + k, me.lat_peer(k)) for k in range(1, 8)]
        for copy in more:
            copy.start()
        self.gather += more

    def back_start(self):
        core = self.me.core
        halves = (span(self.full, core * 8 * 208, 8 * 208), span(self.other, core * 1024, 1024))
        self.back = [
            remote(half, half, self.sems, self.base + (22, 37)[j], self.me.twin()) for j, half in enumerate(halves)
        ]
        for copy in self.back:
            copy.start()

    def back_finish(self):
        super().back_finish()
        for copy in self.spread:
            copy.wait_send()


NAMES = (
    "x_in", "c_in", "grid", "g1", "table", "picks_t", "spread", "wide_codes", "pos_codes", "wa", "rep", "heads",
    "order", "heads_t", "rep_t", "wo", "g2", "we", "ws", "spread_t", "picks", "order_t",
)


def block(
    kinds, *refs
):
    count = len(NAMES)
    sources, (edge_hbm, m_hbm, t_hbm, o_hbm) = refs[:count], refs[count : count + 4]
    held = refs[count + 4 : 2 * count + 4]
    (
        tsel, tmask, wt, wall, bias, wide_low, flat,
        xs, cs, scaled_in, inv_in, normed_in, packed, q_stack, scores, attn, attn_low, mixed,
        scaled_mid, inv_mid, normed_mid, big, big2, act, gexp, gres, gmix, m_stack, grad_scores, scores_low,
        gpack, gacc, gconv, gains, d_wide,
        x_out, c_out, push_out, x_got, c_got, edge_out,
        m_pay, m_arrived, m_first, m_second, m_full,
        t_pay, t_arrived, t_first, t_second, t_full, t_other,
        sems, local, loads,
    ) = refs[2 * count + 4 :]
    (
        x_in, c_in, grid, g1, table, picks_t, spread, wide_codes, pos_codes, wa, rep, heads,
        order, heads_t, rep_t, wo, g2, we, ws, spread_t, picks, order_t,
    ) = held
    incoming = [pltpu.make_async_copy(a, b, loads.at[n]) for n, (a, b) in enumerate(zip(sources, held))]
    for copy in incoming:
        copy.start()
    me = Place()
    wait_all = greet(me)
    m_sum = Summed(me, sems, 9, 144, m_pay, m_arrived, m_first, m_second, m_full)
    t_sum = Mixed(me, sems, 32, t_pay, t_arrived, t_first, t_second, t_full, t_other)
    gains[...] = jnp.zeros_like(gains)
    gacc[...] = jnp.zeros_like(gacc)
    edges = [Edges(me, x_out, x_got, sems, 0, -1), Edges(me, c_out, c_got, sems, 3, -1)]
    for copy in incoming[0:3]:
        copy.wait()
    for n, (src, out) in enumerate(((x_in, x_out), (c_in, c_out))):
        spread_pieces(out, dot(grid[...], src[144:432, :]).astype(BF16), 0)
        ends = jnp.concatenate([src[432:576, :], src[0:144, :]], axis=0)
        spread_pieces(out, dot(grid[...], ends).astype(BF16), 1)
        if n == 0:
            wait_all()
        edges[n].start()
    x_got[0:224, :] = x_out[0:224, :]
    c_got[0:224, :] = c_out[0:224, :]
    for copy in incoming[3:]:
        copy.wait()
    prepare_bias(me.lat, kinds, table, pos_codes, wide_codes, spread, picks_t, tmask, wt, wall, bias)
    edges[0].finish()
    for i in range(2):
        xs[i * HALF : (i + 1) * HALF, :] = dot(order[...], gathered_pieces(x_got, i))
    step = 96
    for start in range(0, TOK, step):
        rows = slice(start, start + step)
        scaled, inverse = norm(xs[rows, :])
        scaled_in[rows, :] = scaled
        inv_in[rows, :] = inverse
        normed_in[rows, :] = (scaled * g1[...]).astype(BF16)
    for part in range(3):
        weight = wa[:, part * C : (part + 1) * C]
        packed[part] = dot(normed_in[...], weight).astype(BF16)
    for w in range(4):
        rows = slice(w * WIN, (w + 1) * WIN)
        i = w // 2
        query, key, value = packed[0, rows, :], packed[1, rows, :], packed[2, rows, :]
        q_stack[w] = dot(rep[...], query).astype(BF16) * heads[...]
        scores[...] = dot(key, q_stack[w], NT)
        for lane in range(0, LANESP, 128):
            lanes = slice(lane, lane + 128)
            s = scores[:, lanes] * SCALE + bias[i, :, lanes]
            e = jnp.exp(s - jnp.max(s, axis=0, keepdims=True))
            a = e * (1.0 / jnp.sum(e, axis=0, keepdims=True))
            attn[w, :, lanes] = a
            attn_low[w, :, lanes] = a.astype(BF16)
        value_t = value.astype(F32).T.astype(BF16)
        per_head = dot(value_t, attn_low[w]).astype(BF16) * heads_t[...]
        mixed[rows, :] = dot(rep_t[...], per_head, NT).astype(BF16)
    big2[:, 0:C] = dot(mixed[...], wo[...])
    for start in range(0, TOK, step):
        rows = slice(start, start + step)
        residual = (xs[rows, :] + big2[rows, 0:C]).astype(BF16).astype(F32)
        scaled, inverse = norm(residual)
        scaled_mid[rows, :] = scaled
        inv_mid[rows, :] = inverse
        normed_mid[rows, :] = (scaled * g2[...]).astype(BF16)
    edges[1].finish()
    for i in range(2):
        cs[i * HALF : (i + 1) * HALF, :] = dot(order[...], gathered_pieces(c_got, i)).astype(BF16)
    big[...] = dot(normed_mid[...], we[...])
    big2[...] = dot(cs[...], ws[...])
    for start in range(0, TOK, 16):
        rows = slice(start, start + 16)
        activated, slope = activation(big[rows, :])
        act[rows, :] = activated.astype(BF16)
        gexp[rows, :] = (big2[rows, :] * slope).astype(BF16)
    d_wide[:, 0:HID] = dot(normed_mid[...], gexp[...], TN)
    d_wide[:, HID : 2 * HID] = dot(cs[...], act[...], TN)
    for t in range(12):
        m_sum.pay[t * C : (t + 1) * C, :] = d_wide[:, t * 128 : (t + 1) * 128].astype(BF16)
    m_sum.core_start()
    big[:, 0:C] = dot(gexp[...], we[...], NT)
    gain_sum = jnp.zeros((1, C), F32)
    for start in range(0, TOK, step):
        rows = slice(start, start + step)
        grad = big[rows, 0:C]
        scaled = scaled_mid[rows, :]
        gain_sum = gain_sum + jnp.sum(grad * scaled, axis=0, keepdims=True)
        gres[rows, :] = norm_back(grad * g2[...], scaled, inv_mid[rows, :]) + cs[rows, :].astype(F32)
    gains[1:2, 0:C] = gain_sum
    grad_low = gres[...].astype(BF16)
    d_wide[:, 3 * C : 4 * C] = dot(mixed[...], grad_low, TN)
    gmix[...] = dot(grad_low, wo[...], NT).astype(BF16)
    for w in range(4):
        rows = slice(w * WIN, (w + 1) * WIN)
        i = w // 2
        key, value = packed[1, rows, :], packed[2, rows, :]
        m_stack[...] = dot(rep[...], gmix[rows, :]).astype(BF16) * heads[...]
        gpack[2, rows, :] = dot(attn_low[w], m_stack[...]).astype(BF16)
        if w == 0:
            m_sum.core_finish()
            m_sum.scatter_start()
        scores[...] = dot(value, m_stack[...], NT)
        for lane in range(0, LANESP, 128):
            lanes = slice(lane, lane + 128)
            a = attn[w, :, lanes]
            da = scores[:, lanes]
            ds = a * (da - jnp.sum(da * a, axis=0, keepdims=True))
            scores_low[:, lanes] = (ds * SCALE).astype(BF16)
            if w % 2 == 0:
                grad_scores[:, lanes] = ds
            else:
                grad_scores[:, lanes] = grad_scores[:, lanes] + ds
        gpack[1, rows, :] = dot(scores_low[...], q_stack[w]).astype(BF16)
        key_t = key.astype(F32).T.astype(BF16)
        per_head = dot(key_t, scores_low[...]).astype(BF16) * heads_t[...]
        gpack[0, rows, :] = dot(rep_t[...], per_head, NT).astype(BF16)
        if w % 2 == 1:
            gacc[...] = jnp.zeros_like(gacc)
            for b in range(WLON):
                start = (WLON - 1 - b) * 72
                gacc[0:ZA, start : start + LANES] = (
                    gacc[0:ZA, start : start + LANES] + grad_scores[b * ZA : (b + 1) * ZA, 0:LANES]
                )
            own_head = wide_codes[0:1, :]
            for h in range(HEADS):
                place = (i * HEADS + h) * 16
                wide_low[place : place + 16, :] = jnp.where(own_head == h, gacc[...], 0.0).astype(BF16)
    folded = dot(wide_low[...], spread_t[...]).astype(BF16)
    mine = lax.broadcasted_iota(jnp.int32, (16, POSP), 0) == pos_codes[0:1, :]
    flat[...] = dot(folded, picks[...])
    for k in range(2 * HEADS):
        tsel[k : k + 1, :] = jnp.sum(
            jnp.where(mine, flat[k * 16 : (k + 1) * 16, :], 0.0), axis=0, keepdims=True
        )
    lane = lax.broadcasted_iota(jnp.int32, (1, 128), 1)
    gconv[...] = jnp.zeros_like(gconv)
    for t in range(32):
        if t < 26:
            gconv[t * 16 : t * 16 + ZA, :] = tsel[0:ZA, t * 128 : (t + 1) * 128]
        for i in range(2):
            row = t * 16 + ZA + i
            gconv[row : row + 1, :] = jnp.where(lane == kinds[0, i], 1.0, 0.0)
    for k in range(16):
        t_sum.pay[k * 112 + 80 : k * 112 + 112, :] = gconv[k * 32 : k * 32 + 32, :].astype(BF16)
    back = None
    for part in range(3):
        lanes = slice(part * C, (part + 1) * C)
        d_wide[:, lanes] = dot(normed_in[...], gpack[part], TN)
        term = dot(gpack[part], wa[:, lanes], NT)
        back = term if back is None else back + term
    big[:, 0:C] = back
    for t in range(6):
        put_flat(t_sum.pay, t * C, d_wide[:, t * 128 : (t + 1) * 128].astype(BF16))
    put_flat(t_sum.pay, 6 * C, jnp.zeros((128, 128), BF16))
    gain_sum = jnp.zeros((1, C), F32)
    for start in range(0, TOK, step):
        rows = slice(start, start + step)
        grad = big[rows, 0:C]
        scaled = scaled_in[rows, :]
        gain_sum = gain_sum + jnp.sum(grad * scaled, axis=0, keepdims=True)
        result = norm_back(grad * g1[...], scaled, inv_in[rows, :]) + gres[rows, :]
        act[rows, 0:C] = result.astype(BF16)
    gains[0:1, 0:C] = gain_sum
    put_flat(t_sum.pay, 6 * C, gains[:, 0:128].astype(BF16))
    put_flat(t_sum.pay, 6 * C + 16, gains[:, 128:256].astype(BF16))
    t_sum.core_start()
    m_sum.scatter_finish()
    m_sum.exchange_start()
    for i in range(2):
        pieces = dot(order_t[...], act[i * HALF : (i + 1) * HALF, 0:C]).astype(BF16)
        spread_pieces(push_out, pieces, i)
    edge_out[0:224, :] = push_out[0:224, :]
    push = Edges(me, push_out, edge_out, sems, 6, 1)
    t_sum.core_finish()
    t_sum.scatter_start()
    t_sum.scatter_finish()
    t_sum.exchange_start()
    push.start()
    m_sum.exchange_finish()
    m_sum.gather_start()
    t_sum.exchange_finish()
    t_sum.gather_start()
    outs = [pltpu.make_async_copy(edge_out, edge_hbm, local.at[0])]
    m_sum.gather_finish()
    m_sum.back_start()
    m_sum.back_finish()
    outs.append(pltpu.make_async_copy(m_sum.full, m_hbm, local.at[1]))
    outs[1].start()
    push.finish()
    outs[0].start()
    t_sum.gather_finish()
    t_sum.back_start()
    t_sum.back_finish()
    outs.append(pltpu.make_async_copy(t_sum.full, t_hbm, local.at[2]))
    outs.append(pltpu.make_async_copy(t_sum.other, o_hbm, local.at[3]))
    for copy in outs[2:]:
        copy.start()
    for copy in outs:
        copy.wait()


def summed_scratch(n, second, full):
    return [
        pltpu.VMEM((16 * n, 128), BF16),
        pltpu.VMEM((8 * n, 128), BF16),
        pltpu.VMEM((7, n, 128), BF16),
        pltpu.VMEM((8, second, 128), BF16),
        pltpu.VMEM((16 * full, 128), BF16),
    ]


def local_scratch():
    return [
        pltpu.VMEM((16, POSP), F32),
        pltpu.VMEM((384, POSP), BF16),
        pltpu.VMEM((192, WIDEP), F32),
        pltpu.VMEM((2, 16, WIDEP), F32),
        pltpu.VMEM((2, WIN, LANESP), F32),
        pltpu.VMEM((192, WIDEP), BF16),
        pltpu.VMEM((192, POSP), F32),
        pltpu.VMEM((TOK, C), F32),
        pltpu.VMEM((TOK, C), BF16),
        pltpu.VMEM((TOK, C), F32),
        pltpu.VMEM((TOK, 1), F32),
        pltpu.VMEM((TOK, C), BF16),
        pltpu.VMEM((3, TOK, C), BF16),
        pltpu.VMEM((4, LANESP, C), BF16),
        pltpu.VMEM((WIN, LANESP), F32),
        pltpu.VMEM((4, WIN, LANESP), F32),
        pltpu.VMEM((4, WIN, LANESP), BF16),
        pltpu.VMEM((TOK, C), BF16),
        pltpu.VMEM((TOK, C), F32),
        pltpu.VMEM((TOK, 1), F32),
        pltpu.VMEM((TOK, C), BF16),
        pltpu.VMEM((TOK, HID), F32),
        pltpu.VMEM((TOK, HID), F32),
        pltpu.VMEM((TOK, HID), BF16),
        pltpu.VMEM((TOK, HID), BF16),
        pltpu.VMEM((TOK, C), F32),
        pltpu.VMEM((TOK, C), BF16),
        pltpu.VMEM((LANESP, C), BF16),
        pltpu.VMEM((WIN, LANESP), F32),
        pltpu.VMEM((WIN, LANESP), BF16),
        pltpu.VMEM((3, TOK, C), BF16),
        pltpu.VMEM((16, WIDEP), F32),
        pltpu.VMEM((512, 128), F32),
        pltpu.VMEM((16, 256), F32),
        pltpu.VMEM((C, 2 * HID), F32),
        *[pltpu.VMEM((640, 256), BF16)] * 6,
        *summed_scratch(144, 144, 144),
        *summed_scratch(112, 96, 208),
        pltpu.VMEM((2048, 128), BF16),
        pltpu.SemaphoreType.DMA((2, 72)),
        pltpu.SemaphoreType.DMA((4,)),
        pltpu.SemaphoreType.DMA((len(NAMES),)),
    ]


def final_constants():
    col, row = np.arange(128), np.arange(96)
    same = (row[:, None] // 16 == col[None, :] % 16 % 6) & (col[None, :] % 16 < ZA)
    pick = col[None, :] == (row % 16)[:, None]
    source = np.where(col % 16 < ZA, col // 16 * 16 + ZA + col % 16 // 6, -1)
    share = source[:, None] == col[None, :]
    low = lambda a: jnp.asarray(a.astype(np.float32), BF16)
    return low(same), low(pick / 16.0), low(share)


def finish(
    edge_hbm, m_hbm, t_hbm, o_hbm, grid_hbm, same_hbm, pick_hbm, share_hbm,
    gx_hbm, first_hbm, second_hbm, attend_hbm, output_hbm, expand_hbm, shrink_hbm, table_hbm,
    edge, m, t, other, grid_t, same, pick, share,
    gx, d_first, d_second, d_attend, d_output, d_expand, d_shrink, table, loads, stores,
):
    factor = 1.0 / math.sqrt(TOK * 128)
    pairs = (
        (m_hbm, m), (t_hbm, t), (o_hbm, other), (share_hbm, share), (pick_hbm, pick), (same_hbm, same), (grid_hbm, grid_t),
        (edge_hbm, edge),
    )
    incoming = [pltpu.make_async_copy(src, dst, loads.at[j]) for j, (src, dst) in enumerate(pairs)]
    for copy in incoming:
        copy.start()
    outgoing = []

    def store(src, dst):
        copy = pltpu.make_async_copy(src, dst, stores.at[len(outgoing)])
        copy.start()
        outgoing.append(copy)

    incoming[0].wait()
    for j in range(6):
        d_expand[:, j * 128 : (j + 1) * 128] = m[j * C : (j + 1) * C, :].astype(F32) * factor
    store(d_expand, expand_hbm)
    for j in range(6):
        d_shrink[:, j * 128 : (j + 1) * 128] = m[(j + 6) * C : (j + 7) * C, :].astype(F32) * factor
    store(d_shrink, shrink_hbm)
    for copy in incoming[1:6]:
        copy.wait()

    def near_block(k):
        return t[k * 208 + 80 : k * 208 + 208, :]

    def far_block(k):
        starts = [((k // 8 * 8 + j) * 8 + k % 8) * 16 for j in range(8)]
        return jnp.concatenate([other[at : at + 16, :] for at in starts], axis=0)

    def choice(values):
        kinds = dot(share[...], values).astype(BF16)
        return dot(pick[...], kinds, NT).astype(BF16) * same[...]

    near, far = choice(near_block(0)), (choice(far_block(0)), choice(far_block(4)))
    for k in range(13):
        for o in range(2):
            part = dot(near, near_block(k)) if o == 0 else dot(far[k % 8 // 4], far_block(k))
            lo = (2 * k + o) * 128
            width = min(128, POS - lo)
            for h in range(HEADS):
                table[h, :, lo : lo + width] = part[h * 16 : h * 16 + 16, 0:width]
    store(table, table_hbm)

    def flat(start, n):
        return [
            (done, size, t[share_id * 208 + off : share_id * 208 + off + size, :].astype(F32) * factor)
            for done, size, share_id, off in flat_spans(start, n)
        ]

    for j in range(4):
        for done, size, values in flat(j * C, C):
            d_attend[done : done + size, j * 128 : (j + 1) * 128] = values
    for done, size, values in flat(4 * C, C):
        d_attend[done : done + size, 512:576] = values[:, 0:64]
        d_output[done : done + size, 0:64] = values[:, 64:128]
    store(d_attend, attend_hbm)
    for done, size, values in flat(5 * C, C):
        d_output[done : done + size, 64:192] = values
    store(d_output, output_hbm)
    low, high = flat(6 * C, 16)[0][2], flat(6 * C + 16, 16)[0][2]
    for row, dst, hbm in ((0, d_first, first_hbm), (1, d_second, second_hbm)):
        dst[:, 0:128] = low[row : row + 1, :]
        dst[:, 128:192] = high[row : row + 1, 0:64]
        store(dst, hbm)
    for copy in incoming[6:]:
        copy.wait()
    for i in range(2):
        result = dot(grid_t[...], gathered_pieces(edge, i)).astype(BF16)
        if i == 0:
            gx[144:432, :] = result
        else:
            gx[432:576, :] = result[0:144, :]
            gx[0:144, :] = result[144:288, :]
    store(gx, gx_hbm)
    for copy in outgoing:
        copy.wait()


def body(
    fields, cotangent, window_kinds, first_gain, attend_weight, output_weight,
    second_gain, expand_weight, shrink_weight, bias_table,
):
    hbm = pl.BlockSpec(memory_space=pl.ANY)
    consts = constants()
    named = dict(
        zip(
            ("rep", "rep_t", "heads", "heads_t", "pos_codes", "wide_codes", "spread", "spread_t", "order", "order_t",
             "grid", "picks", "picks_t"),
            consts,
        ),
        x_in=fields.reshape(TOK, C), c_in=cotangent.reshape(TOK, C), g1=first_gain[None], wa=attend_weight,
        wo=output_weight, g2=second_gain[None], we=expand_weight, ws=shrink_weight.T,
        table=bias_table.transpose(1, 0, 2),
    )
    operands = [named[name] for name in NAMES]
    sent = pl.pallas_call(
        block,
        out_shape=[jax.ShapeDtypeStruct(s, BF16) for s in ((640, 256), (2304, 128), (3328, 128), (2048, 128))],
        in_specs=[pl.BlockSpec(memory_space=pltpu.SMEM)] + [hbm] * len(NAMES),
        out_specs=[hbm] * 4,
        scratch_shapes=[pltpu.VMEM(a.shape, a.dtype) for a in operands] + local_scratch(),
        compiler_params=pltpu.CompilerParams(
            vmem_limit_bytes=60 * 2**20, collective_id=0, has_side_effects=True
        ),
        name="block_backward",
    )(window_kinds.T, *operands)
    shapes = [
        ((TOK, C), BF16), ((1, C), F32), ((1, C), F32), ((C, 3 * C), F32), ((C, C), F32),
        ((C, HID), F32), ((C, HID), F32), ((HEADS, TYPES, POS), F32),
    ]
    inputs = [*sent, named["grid"].T, *final_constants()]
    gx, d_first, d_second, d_attend, d_output, d_expand, d_shrink, table = pl.pallas_call(
        finish,
        out_shape=[jax.ShapeDtypeStruct(s, d) for s, d in shapes],
        in_specs=[hbm] * 8,
        out_specs=[hbm] * 8,
        scratch_shapes=[
            *[pltpu.VMEM(a.shape, BF16) for a in inputs], *[pltpu.VMEM(s, d) for s, d in shapes],
            pltpu.SemaphoreType.DMA((8,)), pltpu.SemaphoreType.DMA((8,)),
        ],
        compiler_params=pltpu.CompilerParams(vmem_limit_bytes=60 * 2**20),
        name="finish",
    )(*inputs)
    return (
        gx.reshape(LEV, ROWS, COLS, C), d_first[0], d_attend, d_output, d_second[0],
        d_expand, d_shrink.T, table.transpose(1, 0, 2),
    )


def solution(mesh):
    cells = P(None, "lat", "lon", None)
    in_specs = (cells, cells, P(None, "lat")) + (P(),) * 7
    out_specs = (cells,) + (P(),) * 7
    return jax.shard_map(body, mesh=mesh, in_specs=in_specs, out_specs=out_specs, check_vma=False)
```

```python
import functools
import math

import jax
import jax.numpy as jnp
import numpy as np
from jax import lax
from jax.experimental import pallas as pl
from jax.experimental.pallas import tpu as pltpu
from jax.sharding import PartitionSpec as P

F32, BF16 = jnp.float32, jnp.bfloat16
C, HEADS, HID = 192, 6, 768
WZ, WLAT, WLON = 2, 6, 12
LEV, ROWS, COLS = 4, 6, 24
POS, POSP = 3312, 3328
TYPES = 16
WIN = WZ * WLAT * WLON
ZA = WZ * WLAT
DIFFS = 2 * WLON - 1
LANES, LANESP = HEADS * WIN, 896
WIDE, WIDEP = DIFFS * HEADS * ZA, 1664
CODES, CODESP = DIFFS * ZA, 288
TOK = LEV * ROWS * COLS
HALF = TOK // 2
SCALE = (C // HEADS) ** (-0.5)
EPS = 1e-05


def constants():
    lane = np.arange(LANESP)
    lane_b, lane_h, lane_za = lane // 72, (lane // 12) % 6, lane % 12
    real = lane < LANES
    rep = ((lane_b * 12 + lane_za)[:, None] == np.arange(WIN)[None, :]) & real[:, None]
    heads = (lane_h[:, None] == (np.arange(C) // 32)[None, :]) & real[:, None]
    pos = np.arange(POSP)
    diff, rest = pos % DIFFS, pos // DIFFS
    aq, ap, zq, zp = rest % 6, rest // 6 % 6, rest // 36 % 2, rest // 72
    fine = pos < POS
    code = np.where(fine, diff * ZA + zp * 6 + ap, -1)
    rho = np.where(fine, zq * 6 + aq, -1)
    pos_codes = rho[None, :].astype(np.int32)
    picks = np.arange(CODESP)[:, None] == code[None, :]
    wide = np.arange(WIDEP)
    wide_r, wide_h, wide_za = wide // 72, (wide // 12) % 6, wide % 12
    okay = wide < WIDE
    spread = ((wide_r * 12 + wide_za)[None, :] == np.arange(CODESP)[:, None]) & okay[None, :]
    wide_codes = np.stack(
        [np.where(okay, wide_h, -1), wide_za // 6, (wide_za % 6) // 3]
    ).astype(np.int32)
    cell = np.arange(HALF)
    lon, z, a = cell // ZA, cell % ZA // 6, cell % 6
    place = np.where(
        a < 3,
        np.where(lon < 18, (z * 3 + a) * 18 + lon, 112 + (z * 3 + a) * 6 + lon - 18),
        np.where(lon < 18, 160 + (z * 3 + a - 3) * 18 + lon, 272 + (z * 3 + a - 3) * 6 + lon - 18),
    )
    order = place[:, None] == np.arange(320)[None, :]
    z, a, lon = cell // 144, cell % 144 // 24, cell % 24
    place = np.where(
        a >= 3,
        np.where(lon >= 6, (z * 3 + a - 3) * 18 + lon - 6, 112 + (z * 3 + a - 3) * 6 + lon),
        np.where(lon >= 6, 160 + (z * 3 + a) * 18 + lon - 6, 272 + (z * 3 + a) * 6 + lon),
    )
    grid = np.arange(320)[:, None] == place[None, :]
    low = lambda a: jnp.asarray(a.astype(np.float32), BF16)
    return (
        low(rep), low(rep.T), low(heads), low(heads.T),
        jnp.asarray(pos_codes), jnp.asarray(wide_codes), low(spread), low(spread.T), low(order), low(order.T), low(grid),
        low(picks), low(picks.T),
    )


def dot(a, b, dims=((1,), (0,))):
    return lax.dot_general(a, b, (dims, ((), ())), preferred_element_type=F32)


NT = ((1,), (1,))
TN = ((0,), (0,))


def split2(v):
    hi = v.astype(BF16)
    return hi, (v - hi.astype(F32)).astype(BF16)


def norm(values):
    center = values - jnp.mean(values, axis=-1, keepdims=True)
    inverse = lax.rsqrt(jnp.mean(center * center, axis=-1, keepdims=True) + EPS)
    return center * inverse, inverse


def norm_back(weighted, scaled, inverse):
    return inverse * (
        weighted
        - jnp.mean(weighted, axis=-1, keepdims=True)
        - scaled * jnp.mean(weighted * scaled, axis=-1, keepdims=True)
    )


def activation(values):
    normal_cdf = 0.5 * (1.0 + lax.erf(values * 0.7071067811865476))
    density = jnp.exp(-0.5 * values * values) * 0.3989422804014327
    return values * normal_cdf, normal_cdf + values * density


def prepare_bias(lat, kinds, table, pos_codes, wide_codes, spread, picks_t, tmask, wt, wall, bias):
    mine = lax.broadcasted_iota(jnp.int32, (16, POS), 0) == pos_codes[0:1, 0:POS]
    tmask[:, 3200:POSP] = jnp.zeros((2 * 192, 128), BF16)
    for i in range(2):
        for h in range(HEADS):
            values = table[h, pl.ds(kinds[0, i], 1), :]
            k = i * HEADS + h
            high = values.astype(BF16).astype(F32)
            for part, piece in enumerate((high, values - high)):
                start = part * 192 + k * 16
                tmask[start : start + 16, 0:POS] = jnp.where(mine, piece, 0.0).astype(BF16)
    both = dot(tmask[...], picks_t[...])
    coded = both[0:192, :] + both[192:384, :]
    both = dot(jnp.concatenate(split2(coded), axis=0), spread[...])
    wt[...] = both[0:192, :] + both[192:384, :]
    own_head = wide_codes[0:1, :]
    row_id = lax.broadcasted_iota(jnp.int32, (ZA, WIDEP), 0)
    row_z = (row_id >= 6).astype(jnp.int32)
    row_a = row_id - 6 * row_z
    level_cut = row_z != wide_codes[1:2, :]
    row_cut = (row_a >= 3).astype(jnp.int32) != wide_codes[2:3, :]
    last = jnp.full((ZA, WIDEP), lat, jnp.int32) == lax.axis_size("lat") - 1
    bias[...] = jnp.zeros_like(bias)
    for i in range(2):
        acc = jnp.zeros((ZA, WIDEP), F32)
        for h in range(HEADS):
            start = (i * HEADS + h) * 16
            acc = acc + jnp.where(own_head == h, wt[start : start + ZA, :], 0.0)
        cut = row_cut & last
        if i == 1:
            cut = cut | level_cut
        wall[i, 0:ZA, :] = jnp.where(cut, -1e30, acc)
        for b in range(WLON):
            start = (WLON - 1 - b) * 72
            bias[i, b * ZA : (b + 1) * ZA, 0:LANES] = wall[i, 0:ZA, start : start + LANES]


MESH = pl.DeviceIdType.MESH


class Place:
    def __init__(self):
        self.lon, self.lat = lax.axis_index("lon"), lax.axis_index("lat")
        self.core = lax.rem(self.lon, 2)
        self.ring = lax.div(self.lon, 2)

    def twin(self):
        return (self.lon + 1 - 2 * self.core, self.lat)

    def ring_at(self, k):
        return lax.rem(self.ring + k, 8)

    def ring_peer(self, k):
        return (self.ring_at(k) * 2 + self.core, self.lat)

    def fold_lat(self, k):
        near = lax.div(self.ring_at(k), 4) == lax.div(self.ring, 4)
        return jnp.where(near, self.lat, self.lat + 1 - 2 * lax.rem(self.lat, 2))

    def fold_peer(self, k):
        return (self.ring_at(k) * 2 + self.core, self.fold_lat(k))

    def lat_peer(self, k):
        return (self.lon, lax.rem(self.lat + k, 8))

    def beside(self, east, north):
        return (lax.rem(self.lon + 16 + east, 16), lax.rem(self.lat + 8 + north, 8))


def greet(me):
    others = [me.twin()]
    others += [me.ring_peer(k) for k in range(1, 8)] + [me.lat_peer(k) for k in range(1, 8)]
    others += [me.fold_peer(k) for k in range(1, 8)]
    others += [me.beside(1, 0), me.beside(-1, 0), me.beside(1, 1), me.beside(-1, -1)]
    barrier = pltpu.get_barrier_semaphore()
    for other in others:
        pl.semaphore_signal(barrier, inc=1, device_id=other, device_id_type=MESH)
    return lambda: pl.semaphore_wait(barrier, len(others))


def remote(src, dst, sems, index, device):
    return pltpu.make_async_remote_copy(
        src_ref=src, dst_ref=dst, send_sem=sems.at[0, index], recv_sem=sems.at[1, index],
        device_id=device, device_id_type=MESH,
    )


class Edges:
    def __init__(self, me, src, dst, sems, base, by):
        pieces = ((224, 320, (by, 0)), (320, 544, (0, by)), (544, 640, (by, by)))
        self.copies = [
            remote(src.at[pl.ds(lo, hi - lo)], dst.at[pl.ds(lo, hi - lo)], sems, base + j, me.beside(*way))
            for j, (lo, hi, way) in enumerate(pieces)
        ]

    def start(self):
        for copy in self.copies:
            copy.start()

    def finish(self):
        for copy in self.copies:
            copy.wait()


EDGE_PARTS = ((0, 112, 0), (112, 160, 224), (160, 272, 320), (272, 320, 544))


def spread_pieces(dst, pieces, i):
    for lo, hi, base in EDGE_PARTS:
        n = hi - lo
        dst[base + i * n : base + (i + 1) * n, 0:C] = pieces[lo:hi, :]


def gathered_pieces(src, i):
    return jnp.concatenate(
        [src[base + i * (hi - lo) : base + (i + 1) * (hi - lo), 0:C] for lo, hi, base in EDGE_PARTS], axis=0
    )


def flat_spans(start, n):
    done = 0
    while done < n:
        share, off = divmod(start + done, 80)
        size = min(80 - off, n - done)
        yield done, size, share, off
        done += size


def put_flat(pay, start, values):
    for done, size, share, off in flat_spans(start, values.shape[0]):
        pay[share * 112 + off : share * 112 + off + size, :] = values[done : done + size, :]


def span(ref, start, n):
    return ref.at[pl.ds(pl.multiple_of(start, 16), n)]


class Summed:
    def __init__(self, me, sems, base, n, pay, arrived, first, second, full):
        self.me, self.sems, self.base, self.n = me, sems, base, n
        self.pay, self.arrived, self.first, self.second, self.full = pay, arrived, first, second, full

    def core_start(self):
        n = self.n
        self.core_copy = remote(
            span(self.pay, (1 - self.me.core) * 8 * n, 8 * n), self.arrived, self.sems, self.base, self.me.twin()
        )
        self.core_copy.start()

    def core_finish(self):
        self.core_copy.wait()
        n = self.n
        for s in range(8):
            place = pl.ds(pl.multiple_of(self.me.core * 8 * n + s * n, 16), n)
            mine = self.pay[place, :].astype(F32) + self.arrived[s * n : (s + 1) * n, :].astype(F32)
            self.pay[place, :] = mine.astype(BF16)

    def first_peer(self, k):
        return self.me.fold_peer(k)

    def scatter_start(self):
        me, n = self.me, self.n
        self.scatter = [
            remote(
                span(self.pay, (me.core * 8 + me.ring_at(k)) * n, n), self.first.at[k - 1],
                self.sems, self.base + k, self.first_peer(k),
            )
            for k in range(1, 8)
        ]
        for copy in self.scatter:
            copy.start()

    def scattered(self):
        me, n = self.me, self.n
        total = self.pay[pl.ds(pl.multiple_of((me.core * 8 + me.ring) * n, 16), n), :].astype(F32)
        for copy in self.scatter:
            copy.wait_recv()
        for k in range(7):
            total = total + self.first[k].astype(F32)
        return total.astype(BF16)

    def scatter_finish(self):
        self.second[self.me.lat] = self.scattered()

    def exchange_start(self):
        me = self.me
        self.exchange = [
            remote(self.second.at[me.lat], self.second.at[me.lat], self.sems, self.base + 7 + k, me.lat_peer(k))
            for k in range(1, 8)
        ]
        for copy in self.exchange:
            copy.start()

    def exchanged(self, summed):
        for copy in self.exchange:
            copy.wait_recv()
        total = self.second[0, 0:summed, :].astype(F32)
        for k in range(1, 8):
            total = total + self.second[k, 0:summed, :].astype(F32)
        return total.astype(BF16)

    def exchange_finish(self):
        me, n = self.me, self.n
        self.full[pl.ds(pl.multiple_of((me.core * 8 + me.ring) * n, 16), n), :] = self.exchanged(n)

    def gather_start(self):
        me, n = self.me, self.n
        own = span(self.full, (me.core * 8 + me.ring) * n, n)
        self.gather = [
            remote(own, own, self.sems, self.base + 14 + k, me.fold_peer(k)) for k in range(1, 8)
        ]
        for copy in self.gather:
            copy.start()

    def gather_finish(self):
        for copy in self.gather:
            copy.wait_recv()

    def back_start(self):
        half = span(self.full, self.me.core * 8 * self.n, 8 * self.n)
        self.back = [remote(half, half, self.sems, self.base + 22, self.me.twin())]
        self.back[0].start()

    def back_finish(self):
        for copy in self.back:
            copy.wait()
        for copy in self.scatter + self.exchange + self.gather:
            copy.wait_send()


class Mixed(Summed):
    def __init__(self, me, sems, base, pay, arrived, first, second, full, other):
        super().__init__(me, sems, base, 112, pay, arrived, first, second, full)
        self.other = other

    def first_peer(self, k):
        return self.me.ring_peer(k)

    def other_at(self, lat):
        return ((self.me.core * 8 + lat) * 8 + self.me.ring) * 16

    def scatter_finish(self):
        total = self.scattered()
        self.second[self.me.lat] = total[0:96, :]
        self.other[pl.ds(pl.multiple_of(self.other_at(self.me.lat), 16), 16), :] = total[96:112, :]

    def exchange_start(self):
        me = self.me
        super().exchange_start()
        self.spread = [
            remote(
                span(self.other, self.other_at(me.lat), 16), span(self.other, self.other_at(me.fold_lat(k)), 16),
                self.sems, self.base + 22 + k, me.fold_peer(k),
            )
            for k in range(1, 8)
        ]
        for copy in self.spread:
            copy.start()

    def exchange_finish(self):
        me = self.me
        start = (me.core * 8 + me.ring) * 208
        self.full[pl.ds(pl.multiple_of(start, 16), 80), :] = self.exchanged(80)
        for k in range(8):
            self.full[pl.ds(pl.multiple_of(start + 80 + k * 16, 16), 16), :] = self.second[k, 80:96, :]

    def gather_start(self):
        me = self.me
        own = span(self.full, (me.core * 8 + me.ring) * 208, 208)
        self.gather = [
            remote(own, own, self.sems, self.base + 14 + k, me.fold_peer(k)) for k in range(1, 8)
        ]
        for copy in self.gather:
            copy.start()
        for copy in self.spread:
            copy.wait_recv()
        mine = span(self.other, (me.core * 8 + me.lat) * 128, 128)
        more = [remote(mine, mine, self.sems, self.base + 29 + k, me.lat_peer(k)) for k in range(1, 8)]
        for copy in more:
            copy.start()
        self.gather += more

    def back_start(self):
        core = self.me.core
        halves = (span(self.full, core * 8 * 208, 8 * 208), span(self.other, core * 1024, 1024))
        self.back = [
            remote(half, half, self.sems, self.base + (22, 37)[j], self.me.twin()) for j, half in enumerate(halves)
        ]
        for copy in self.back:
            copy.start()

    def back_finish(self):
        super().back_finish()
        for copy in self.spread:
            copy.wait_send()


NAMES = (
    "x_in", "c_in", "grid", "g1", "table", "picks_t", "spread", "wide_codes", "pos_codes", "wa", "rep", "heads",
    "order", "heads_t", "rep_t", "wo", "g2", "we", "ws", "spread_t", "picks", "order_t",
)


def block(
    kinds, *refs
):
    count = len(NAMES)
    sources, (edge_hbm, m_hbm, t_hbm, o_hbm) = refs[:count], refs[count : count + 4]
    held = refs[count + 4 : 2 * count + 4]
    (
        tsel, tmask, wt, wall, bias, wide_low, flat,
        xs, cs, scaled_in, inv_in, normed_in, packed, q_stack, scores, attn, attn_low, mixed,
        scaled_mid, inv_mid, normed_mid, big, big2, act, gexp, gres, gmix, m_stack, grad_scores, scores_low,
        gpack, gacc, gconv, gains, d_wide,
        x_out, c_out, push_out, x_got, c_got, edge_out,
        m_pay, m_arrived, m_first, m_second, m_full,
        t_pay, t_arrived, t_first, t_second, t_full, t_other,
        sems, local, loads,
    ) = refs[2 * count + 4 :]
    (
        x_in, c_in, grid, g1, table, picks_t, spread, wide_codes, pos_codes, wa, rep, heads,
        order, heads_t, rep_t, wo, g2, we, ws, spread_t, picks, order_t,
    ) = held
    incoming = [pltpu.make_async_copy(a, b, loads.at[n]) for n, (a, b) in enumerate(zip(sources, held))]
    for copy in incoming:
        copy.start()
    me = Place()
    wait_all = greet(me)
    m_sum = Summed(me, sems, 9, 144, m_pay, m_arrived, m_first, m_second, m_full)
    t_sum = Mixed(me, sems, 32, t_pay, t_arrived, t_first, t_second, t_full, t_other)
    gains[...] = jnp.zeros_like(gains)
    gacc[...] = jnp.zeros_like(gacc)
    edges = [Edges(me, x_out, x_got, sems, 0, -1), Edges(me, c_out, c_got, sems, 3, -1)]
    for copy in incoming[0:3]:
        copy.wait()
    for n, (src, out) in enumerate(((x_in, x_out), (c_in, c_out))):
        spread_pieces(out, dot(grid[...], src[144:432, :]).astype(BF16), 0)
        ends = jnp.concatenate([src[432:576, :], src[0:144, :]], axis=0)
        spread_pieces(out, dot(grid[...], ends).astype(BF16), 1)
        if n == 0:
            wait_all()
            edges[0].start()
    x_got[0:224, :] = x_out[0:224, :]
    c_got[0:224, :] = c_out[0:224, :]
    for copy in incoming[3:]:
        copy.wait()
    prepare_bias(me.lat, kinds, table, pos_codes, wide_codes, spread, picks_t, tmask, wt, wall, bias)
    edges[0].finish()
    edges[1].start()
    for i in range(2):
        xs[i * HALF : (i + 1) * HALF, :] = dot(order[...], gathered_pieces(x_got, i))
    step = 96
    for start in range(0, TOK, step):
        rows = slice(start, start + step)
        scaled, inverse = norm(xs[rows, :])
        scaled_in[rows, :] = scaled
        inv_in[rows, :] = inverse
        normed_in[rows, :] = (scaled * g1[...]).astype(BF16)
    for part in range(3):
        weight = wa[:, part * C : (part + 1) * C]
        packed[part] = dot(normed_in[...], weight).astype(BF16)
    for w in range(4):
        rows = slice(w * WIN, (w + 1) * WIN)
        i = w // 2
        query, key, value = packed[0, rows, :], packed[1, rows, :], packed[2, rows, :]
        q_stack[w] = dot(rep[...], query).astype(BF16) * heads[...]
        scores[...] = dot(key, q_stack[w], NT)
        for lane in range(0, LANESP, 128):
            lanes = slice(lane, lane + 128)
            s = scores[:, lanes] * SCALE + bias[i, :, lanes]
            e = jnp.exp(s - jnp.max(s, axis=0, keepdims=True))
            a = e * (1.0 / jnp.sum(e, axis=0, keepdims=True))
            attn[w, :, lanes] = a
            attn_low[w, :, lanes] = a.astype(BF16)
        value_t = value.astype(F32).T.astype(BF16)
        per_head = dot(value_t, attn_low[w]).astype(BF16) * heads_t[...]
        mixed[rows, :] = dot(rep_t[...], per_head, NT).astype(BF16)
    big2[:, 0:C] = dot(mixed[...], wo[...])
    for start in range(0, TOK, step):
        rows = slice(start, start + step)
        residual = (xs[rows, :] + big2[rows, 0:C]).astype(BF16).astype(F32)
        scaled, inverse = norm(residual)
        scaled_mid[rows, :] = scaled
        inv_mid[rows, :] = inverse
        normed_mid[rows, :] = (scaled * g2[...]).astype(BF16)
    edges[1].finish()
    for i in range(2):
        cs[i * HALF : (i + 1) * HALF, :] = dot(order[...], gathered_pieces(c_got, i)).astype(BF16)
    big[...] = dot(normed_mid[...], we[...])
    big2[...] = dot(cs[...], ws[...])
    for start in range(0, TOK, 16):
        rows = slice(start, start + 16)
        activated, slope = activation(big[rows, :])
        act[rows, :] = activated.astype(BF16)
        gexp[rows, :] = (big2[rows, :] * slope).astype(BF16)
    d_wide[:, 0:HID] = dot(normed_mid[...], gexp[...], TN)
    d_wide[:, HID : 2 * HID] = dot(cs[...], act[...], TN)
    for t in range(12):
        m_sum.pay[t * C : (t + 1) * C, :] = d_wide[:, t * 128 : (t + 1) * 128].astype(BF16)
    m_sum.core_start()
    big[:, 0:C] = dot(gexp[...], we[...], NT)
    gain_sum = jnp.zeros((1, C), F32)
    for start in range(0, TOK, step):
        rows = slice(start, start + step)
        grad = big[rows, 0:C]
        scaled = scaled_mid[rows, :]
        gain_sum = gain_sum + jnp.sum(grad * scaled, axis=0, keepdims=True)
        gres[rows, :] = norm_back(grad * g2[...], scaled, inv_mid[rows, :]) + cs[rows, :].astype(F32)
    gains[1:2, 0:C] = gain_sum
    grad_low = gres[...].astype(BF16)
    d_wide[:, 3 * C : 4 * C] = dot(mixed[...], grad_low, TN)
    gmix[...] = dot(grad_low, wo[...], NT).astype(BF16)
    for w in range(4):
        rows = slice(w * WIN, (w + 1) * WIN)
        i = w // 2
        key, value = packed[1, rows, :], packed[2, rows, :]
        m_stack[...] = dot(rep[...], gmix[rows, :]).astype(BF16) * heads[...]
        gpack[2, rows, :] = dot(attn_low[w], m_stack[...]).astype(BF16)
        if w == 0:
            m_sum.core_finish()
            m_sum.scatter_start()
        scores[...] = dot(value, m_stack[...], NT)
        for lane in range(0, LANESP, 128):
            lanes = slice(lane, lane + 128)
            a = attn[w, :, lanes]
            da = scores[:, lanes]
            ds = a * (da - jnp.sum(da * a, axis=0, keepdims=True))
            scores_low[:, lanes] = (ds * SCALE).astype(BF16)
            if w % 2 == 0:
                grad_scores[:, lanes] = ds
            else:
                grad_scores[:, lanes] = grad_scores[:, lanes] + ds
        gpack[1, rows, :] = dot(scores_low[...], q_stack[w]).astype(BF16)
        key_t = key.astype(F32).T.astype(BF16)
        per_head = dot(key_t, scores_low[...]).astype(BF16) * heads_t[...]
        gpack[0, rows, :] = dot(rep_t[...], per_head, NT).astype(BF16)
        if w % 2 == 1:
            gacc[...] = jnp.zeros_like(gacc)
            for b in range(WLON):
                start = (WLON - 1 - b) * 72
                gacc[0:ZA, start : start + LANES] = (
                    gacc[0:ZA, start : start + LANES] + grad_scores[b * ZA : (b + 1) * ZA, 0:LANES]
                )
            own_head = wide_codes[0:1, :]
            for h in range(HEADS):
                place = (i * HEADS + h) * 16
                wide_low[place : place + 16, :] = jnp.where(own_head == h, gacc[...], 0.0).astype(BF16)
    folded = dot(wide_low[...], spread_t[...]).astype(BF16)
    mine = lax.broadcasted_iota(jnp.int32, (16, POSP), 0) == pos_codes[0:1, :]
    flat[...] = dot(folded, picks[...])
    for k in range(2 * HEADS):
        tsel[k : k + 1, :] = jnp.sum(
            jnp.where(mine, flat[k * 16 : (k + 1) * 16, :], 0.0), axis=0, keepdims=True
        )
    lane = lax.broadcasted_iota(jnp.int32, (1, 128), 1)
    gconv[...] = jnp.zeros_like(gconv)
    for t in range(32):
        if t < 26:
            gconv[t * 16 : t * 16 + ZA, :] = tsel[0:ZA, t * 128 : (t + 1) * 128]
        for i in range(2):
            row = t * 16 + ZA + i
            gconv[row : row + 1, :] = jnp.where(lane == kinds[0, i], 1.0, 0.0)
    for k in range(16):
        t_sum.pay[k * 112 + 80 : k * 112 + 112, :] = gconv[k * 32 : k * 32 + 32, :].astype(BF16)
    back = None
    for part in range(3):
        lanes = slice(part * C, (part + 1) * C)
        d_wide[:, lanes] = dot(normed_in[...], gpack[part], TN)
        term = dot(gpack[part], wa[:, lanes], NT)
        back = term if back is None else back + term
    big[:, 0:C] = back
    for t in range(6):
        put_flat(t_sum.pay, t * C, d_wide[:, t * 128 : (t + 1) * 128].astype(BF16))
    put_flat(t_sum.pay, 6 * C, jnp.zeros((128, 128), BF16))
    gain_sum = jnp.zeros((1, C), F32)
    for start in range(0, TOK, step):
        rows = slice(start, start + step)
        grad = big[rows, 0:C]
        scaled = scaled_in[rows, :]
        gain_sum = gain_sum + jnp.sum(grad * scaled, axis=0, keepdims=True)
        result = norm_back(grad * g1[...], scaled, inv_in[rows, :]) + gres[rows, :]
        act[rows, 0:C] = result.astype(BF16)
    gains[0:1, 0:C] = gain_sum
    put_flat(t_sum.pay, 6 * C, gains[:, 0:128].astype(BF16))
    put_flat(t_sum.pay, 6 * C + 16, gains[:, 128:256].astype(BF16))
    t_sum.core_start()
    m_sum.scatter_finish()
    m_sum.exchange_start()
    for i in range(2):
        pieces = dot(order_t[...], act[i * HALF : (i + 1) * HALF, 0:C]).astype(BF16)
        spread_pieces(push_out, pieces, i)
    edge_out[0:224, :] = push_out[0:224, :]
    push = Edges(me, push_out, edge_out, sems, 6, 1)
    t_sum.core_finish()
    t_sum.scatter_start()
    t_sum.scatter_finish()
    t_sum.exchange_start()
    push.start()
    m_sum.exchange_finish()
    m_sum.gather_start()
    t_sum.exchange_finish()
    t_sum.gather_start()
    outs = [pltpu.make_async_copy(edge_out, edge_hbm, local.at[0])]
    m_sum.gather_finish()
    m_sum.back_start()
    m_sum.back_finish()
    outs.append(pltpu.make_async_copy(m_sum.full, m_hbm, local.at[1]))
    outs[1].start()
    push.finish()
    outs[0].start()
    t_sum.gather_finish()
    t_sum.back_start()
    t_sum.back_finish()
    outs.append(pltpu.make_async_copy(t_sum.full, t_hbm, local.at[2]))
    outs.append(pltpu.make_async_copy(t_sum.other, o_hbm, local.at[3]))
    for copy in outs[2:]:
        copy.start()
    for copy in outs:
        copy.wait()


def summed_scratch(n, second, full):
    return [
        pltpu.VMEM((16 * n, 128), BF16),
        pltpu.VMEM((8 * n, 128), BF16),
        pltpu.VMEM((7, n, 128), BF16),
        pltpu.VMEM((8, second, 128), BF16),
        pltpu.VMEM((16 * full, 128), BF16),
    ]


def local_scratch():
    return [
        pltpu.VMEM((16, POSP), F32),
        pltpu.VMEM((384, POSP), BF16),
        pltpu.VMEM((192, WIDEP), F32),
        pltpu.VMEM((2, 16, WIDEP), F32),
        pltpu.VMEM((2, WIN, LANESP), F32),
        pltpu.VMEM((192, WIDEP), BF16),
        pltpu.VMEM((192, POSP), F32),
        pltpu.VMEM((TOK, C), F32),
        pltpu.VMEM((TOK, C), BF16),
        pltpu.VMEM((TOK, C), F32),
        pltpu.VMEM((TOK, 1), F32),
        pltpu.VMEM((TOK, C), BF16),
        pltpu.VMEM((3, TOK, C), BF16),
        pltpu.VMEM((4, LANESP, C), BF16),
        pltpu.VMEM((WIN, LANESP), F32),
        pltpu.VMEM((4, WIN, LANESP), F32),
        pltpu.VMEM((4, WIN, LANESP), BF16),
        pltpu.VMEM((TOK, C), BF16),
        pltpu.VMEM((TOK, C), F32),
        pltpu.VMEM((TOK, 1), F32),
        pltpu.VMEM((TOK, C), BF16),
        pltpu.VMEM((TOK, HID), F32),
        pltpu.VMEM((TOK, HID), F32),
        pltpu.VMEM((TOK, HID), BF16),
        pltpu.VMEM((TOK, HID), BF16),
        pltpu.VMEM((TOK, C), F32),
        pltpu.VMEM((TOK, C), BF16),
        pltpu.VMEM((LANESP, C), BF16),
        pltpu.VMEM((WIN, LANESP), F32),
        pltpu.VMEM((WIN, LANESP), BF16),
        pltpu.VMEM((3, TOK, C), BF16),
        pltpu.VMEM((16, WIDEP), F32),
        pltpu.VMEM((512, 128), F32),
        pltpu.VMEM((16, 256), F32),
        pltpu.VMEM((C, 2 * HID), F32),
        *[pltpu.VMEM((640, 256), BF16)] * 6,
        *summed_scratch(144, 144, 144),
        *summed_scratch(112, 96, 208),
        pltpu.VMEM((2048, 128), BF16),
        pltpu.SemaphoreType.DMA((2, 72)),
        pltpu.SemaphoreType.DMA((4,)),
        pltpu.SemaphoreType.DMA((len(NAMES),)),
    ]


def final_constants():
    col, row = np.arange(128), np.arange(96)
    same = (row[:, None] // 16 == col[None, :] % 16 % 6) & (col[None, :] % 16 < ZA)
    pick = col[None, :] == (row % 16)[:, None]
    source = np.where(col % 16 < ZA, col // 16 * 16 + ZA + col % 16 // 6, -1)
    share = source[:, None] == col[None, :]
    low = lambda a: jnp.asarray(a.astype(np.float32), BF16)
    return low(same), low(pick / 16.0), low(share)


def finish(
    edge_hbm, m_hbm, t_hbm, o_hbm, grid_hbm, same_hbm, pick_hbm, share_hbm,
    gx_hbm, first_hbm, second_hbm, attend_hbm, output_hbm, expand_hbm, shrink_hbm, table_hbm,
    edge, m, t, other, grid_t, same, pick, share,
    gx, d_first, d_second, d_attend, d_output, d_expand, d_shrink, table, loads, stores,
):
    factor = 1.0 / math.sqrt(TOK * 128)
    pairs = (
        (m_hbm, m), (t_hbm, t), (o_hbm, other), (share_hbm, share), (pick_hbm, pick), (same_hbm, same), (grid_hbm, grid_t),
        (edge_hbm, edge),
    )
    incoming = [pltpu.make_async_copy(src, dst, loads.at[j]) for j, (src, dst) in enumerate(pairs)]
    for copy in incoming:
        copy.start()
    outgoing = []

    def store(src, dst):
        copy = pltpu.make_async_copy(src, dst, stores.at[len(outgoing)])
        copy.start()
        outgoing.append(copy)

    incoming[0].wait()
    for j in range(6):
        d_expand[:, j * 128 : (j + 1) * 128] = m[j * C : (j + 1) * C, :].astype(F32) * factor
    store(d_expand, expand_hbm)
    for j in range(6):
        d_shrink[:, j * 128 : (j + 1) * 128] = m[(j + 6) * C : (j + 7) * C, :].astype(F32) * factor
    store(d_shrink, shrink_hbm)
    for copy in incoming[1:6]:
        copy.wait()

    def near_block(k):
        return t[k * 208 + 80 : k * 208 + 208, :]

    def far_block(k):
        starts = [((k // 8 * 8 + j) * 8 + k % 8) * 16 for j in range(8)]
        return jnp.concatenate([other[at : at + 16, :] for at in starts], axis=0)

    def choice(values):
        kinds = dot(share[...], values).astype(BF16)
        return dot(pick[...], kinds, NT).astype(BF16) * same[...]

    near, far = choice(near_block(0)), (choice(far_block(0)), choice(far_block(4)))
    for k in range(13):
        for o in range(2):
            part = dot(near, near_block(k)) if o == 0 else dot(far[k % 8 // 4], far_block(k))
            lo = (2 * k + o) * 128
            width = min(128, POS - lo)
            for h in range(HEADS):
                table[h, :, lo : lo + width] = part[h * 16 : h * 16 + 16, 0:width]
    store(table, table_hbm)

    def flat(start, n):
        return [
            (done, size, t[share_id * 208 + off : share_id * 208 + off + size, :].astype(F32) * factor)
            for done, size, share_id, off in flat_spans(start, n)
        ]

    for j in range(4):
        for done, size, values in flat(j * C, C):
            d_attend[done : done + size, j * 128 : (j + 1) * 128] = values
    for done, size, values in flat(4 * C, C):
        d_attend[done : done + size, 512:576] = values[:, 0:64]
        d_output[done : done + size, 0:64] = values[:, 64:128]
    store(d_attend, attend_hbm)
    for done, size, values in flat(5 * C, C):
        d_output[done : done + size, 64:192] = values
    store(d_output, output_hbm)
    low, high = flat(6 * C, 16)[0][2], flat(6 * C + 16, 16)[0][2]
    for row, dst, hbm in ((0, d_first, first_hbm), (1, d_second, second_hbm)):
        dst[:, 0:128] = low[row : row + 1, :]
        dst[:, 128:192] = high[row : row + 1, 0:64]
        store(dst, hbm)
    for copy in incoming[6:]:
        copy.wait()
    for i in range(2):
        result = dot(grid_t[...], gathered_pieces(edge, i)).astype(BF16)
        if i == 0:
            gx[144:432, :] = result
        else:
            gx[432:576, :] = result[0:144, :]
            gx[0:144, :] = result[144:288, :]
    store(gx, gx_hbm)
    for copy in outgoing:
        copy.wait()


def body(
    fields, cotangent, window_kinds, first_gain, attend_weight, output_weight,
    second_gain, expand_weight, shrink_weight, bias_table,
):
    hbm = pl.BlockSpec(memory_space=pl.ANY)
    consts = constants()
    named = dict(
        zip(
            ("rep", "rep_t", "heads", "heads_t", "pos_codes", "wide_codes", "spread", "spread_t", "order", "order_t",
             "grid", "picks", "picks_t"),
            consts,
        ),
        x_in=fields.reshape(TOK, C), c_in=cotangent.reshape(TOK, C), g1=first_gain[None], wa=attend_weight,
        wo=output_weight, g2=second_gain[None], we=expand_weight, ws=shrink_weight.T,
        table=bias_table.transpose(1, 0, 2),
    )
    operands = [named[name] for name in NAMES]
    sent = pl.pallas_call(
        block,
        out_shape=[jax.ShapeDtypeStruct(s, BF16) for s in ((640, 256), (2304, 128), (3328, 128), (2048, 128))],
        in_specs=[pl.BlockSpec(memory_space=pltpu.SMEM)] + [hbm] * len(NAMES),
        out_specs=[hbm] * 4,
        scratch_shapes=[pltpu.VMEM(a.shape, a.dtype) for a in operands] + local_scratch(),
        compiler_params=pltpu.CompilerParams(
            vmem_limit_bytes=60 * 2**20, collective_id=0, has_side_effects=True
        ),
        name="block_backward",
    )(window_kinds.T, *operands)
    shapes = [
        ((TOK, C), BF16), ((1, C), F32), ((1, C), F32), ((C, 3 * C), F32), ((C, C), F32),
        ((C, HID), F32), ((C, HID), F32), ((HEADS, TYPES, POS), F32),
    ]
    inputs = [*sent, named["grid"].T, *final_constants()]
    gx, d_first, d_second, d_attend, d_output, d_expand, d_shrink, table = pl.pallas_call(
        finish,
        out_shape=[jax.ShapeDtypeStruct(s, d) for s, d in shapes],
        in_specs=[hbm] * 8,
        out_specs=[hbm] * 8,
        scratch_shapes=[
            *[pltpu.VMEM(a.shape, BF16) for a in inputs], *[pltpu.VMEM(s, d) for s, d in shapes],
            pltpu.SemaphoreType.DMA((8,)), pltpu.SemaphoreType.DMA((8,)),
        ],
        compiler_params=pltpu.CompilerParams(vmem_limit_bytes=60 * 2**20),
        name="finish",
    )(*inputs)
    return (
        gx.reshape(LEV, ROWS, COLS, C), d_first[0], d_attend, d_output, d_second[0],
        d_expand, d_shrink.T, table.transpose(1, 0, 2),
    )


def solution(mesh):
    cells = P(None, "lat", "lon", None)
    in_specs = (cells, cells, P(None, "lat")) + (P(),) * 7
    out_specs = (cells,) + (P(),) * 7
    return jax.shard_map(body, mesh=mesh, in_specs=in_specs, out_specs=out_specs, check_vma=False)
```
